32 devices in a mesh: dp: 4 (over x, core), fsdp: 8 (over z, y).
Axes of the slice: x: 2, y: 2, z: 4, core: 2. Of those that a mesh axis runs over, the one named last changes fastest.
Arguments:
- block_input: bfloat16 [8192, 2048], P(('dp', 'fsdp')), may hold values from -6 to 6
- segment_ids: int32 [8192], P(('dp', 'fsdp')), may hold values from -1 to 3, as said below
- w_query: bfloat16 [2048, 2048], P('fsdp'), may hold values from -0.125 to 0.125
- w_key: bfloat16 [2048, 2048], P('fsdp'), may hold values from -0.125 to 0.125
- w_value: bfloat16 [2048, 2048], P('fsdp'), may hold values from -0.125 to 0.125
- w_out: bfloat16 [2048, 2048], P('fsdp'), may hold values from -0.125 to 0.125
- gain_query: bfloat16 [2048], P('fsdp'), may hold values from 0.25 to 1.75
- gain_key: bfloat16 [2048], P('fsdp'), may hold values from 0.25 to 1.75
- gain_attn: bfloat16 [2048], P('fsdp'), may hold values from 0.25 to 1.75
- w_gate: bfloat16 [2048, 8192], P('fsdp'), may hold values from -0.125 to 0.125
- w_up: bfloat16 [2048, 8192], P('fsdp'), may hold values from -0.125 to 0.125
- w_down: bfloat16 [8192, 2048], P('fsdp'), may hold values from -0.0625 to 0.0625
- gain_mlp: bfloat16 [2048], P('fsdp'), may hold values from 0.25 to 1.75
- out_cotangent: bfloat16 [8192, 2048], P(('dp', 'fsdp')), may hold values from -6 to 6
Outputs:
- block_output: bfloat16 [8192, 2048], P(('dp', 'fsdp'))
- input_grad: float32 [8192, 2048], P(('dp', 'fsdp'))
- grad_w_query: float32 [2048, 2048], P('fsdp')
- grad_w_key: float32 [2048, 2048], P('fsdp')
- grad_w_value: float32 [2048, 2048], P('fsdp')
- grad_w_out: float32 [2048, 2048], P('fsdp')
- grad_gain_query: float32 [2048], P('fsdp')
- grad_gain_key: float32 [2048], P('fsdp')
- grad_gain_attn: float32 [2048], P('fsdp')
- grad_w_gate: float32 [2048, 8192], P('fsdp')
- grad_w_up: float32 [2048, 8192], P('fsdp')
- grad_w_down: float32 [8192, 2048], P('fsdp')
- grad_gain_mlp: float32 [2048], P('fsdp')
The draws below stay inside these ranges and needn't reach their ends.
Inputs may be any that keep to these rules, and one draw needn't show every extreme that they name: `segment_ids`: each aligned block of 128 rows is one micro-batch: its live rows come first with segment ids 0, 1, ... that never fall, each segment contiguous, followed by padding rows of id -1; a micro-batch has 64 or more live rows and at most 4 segments; some micro-batches have no padding.
All inputs are finite; a program needn't handle non-finite values.
Results may differ from the reference program's by a relative error of at most 0.02.
Values may be sent and summed in bfloat16 or wider, within the bound.
No kernel may reach another device: no remote copies, remote signals or barrier semaphores. Data moves between devices by JAX's collectives and lax.ppermute only.
A program may use at most 512 MiB of HBM per device.

```python
import math
import jax
import jax.numpy as jnp
from jax import lax

D = 2048
HEADS = 16
HEAD_DIM = 128
FF = 8192
MB = 128
TOKENS = 8192


def draw_segment_ids(key, part):
    blocks = TOKENS // MB
    key_full, key_many, key_live, key_count, key_cut = jax.random.split(key, 5)
    block_index = jnp.arange(blocks, dtype=jnp.int32)
    full_phase = jax.random.randint(key_full, (), 0, 3)
    many_phase = jax.random.randint(key_many, (), 0, 4)
    live_drawn = jax.random.randint(key_live, (blocks,), MB // 2, MB)
    live_count = jnp.where(block_index % 3 == full_phase, MB, live_drawn)
    count_drawn = jax.random.randint(key_count, (blocks,), 1, 5)
    seg_count = jnp.where(block_index % 4 == many_phase, 4, count_drawn)
    jitter_reach = live_count // (4 * seg_count)
    cut_index = jnp.arange(1, 4, dtype=jnp.int32)
    jitter_raw = jax.random.randint(key_cut, (blocks, 3), 0, 65536)
    jitter = jitter_raw % (2 * jitter_reach[:, None] + 1) - jitter_reach[:, None]
    cut_base = live_count[:, None] * cut_index[None, :] // seg_count[:, None]
    cut_points = jnp.where(cut_index[None, :] < seg_count[:, None], cut_base + jitter, MB + 1)
    position = jnp.arange(MB, dtype=jnp.int32)
    segment_id = jnp.sum((position[None, :, None] >= cut_points[:, None, :]).astype(jnp.int32), axis=2)
    segment_id = jnp.where(position[None, :] < live_count[:, None], segment_id, -1)
    return segment_id.reshape(TOKENS).astype(jnp.int32)


def levels(own_key, shape, cuts, low, largest):
    def one(dim, shards_of):
        heights = jax.random.uniform(jax.random.fold_in(jax.random.fold_in(own_key, 6), dim), (shards_of,), jnp.float32, low / len(cuts), largest / len(cuts))
        return jnp.repeat(jnp.exp(heights), shape[dim] // shards_of).reshape((-1,) + (1,) * (len(shape) - dim - 1))

    loudness = one(*cuts[0])
    for cut in cuts[1:]:
        loudness = loudness * one(*cut)
    return loudness


def normal_values(rng, extent, spread, most, cuts=(), kind=jnp.bfloat16):
    level = levels(rng, extent, cuts, -0.22, 0.18) if cuts else 1.0
    values = jax.random.normal(rng, extent, jnp.float32) * spread * level
    return jnp.minimum(jnp.maximum(values, -most), most).astype(kind)


def setup_inputs(seed: int = 0) -> dict:
    key_list = jax.random.split(jax.random.key(seed), 15)
    return {
        "block_input": normal_values(key_list[0], (TOKENS, D), 1.0, 6.0, ((0, 32),)),
        "segment_ids": draw_segment_ids(jax.random.fold_in(key_list[14], 71), 0),
        "w_query": normal_values(key_list[2], (D, D), D ** -0.5, 0.125, ((0, 8),)),
        "w_key": normal_values(key_list[3], (D, D), D ** -0.5, 0.125, ((0, 8),)),
        "w_value": normal_values(key_list[4], (D, D), D ** -0.5, 0.125, ((0, 8),)),
        "w_out": normal_values(key_list[5], (D, D), D ** -0.5, 0.125, ((0, 8),)),
        "gain_query": jnp.clip(1.0 + 0.15 * jax.random.normal(key_list[6], (D,), jnp.float32), 0.25, 1.75).astype(jnp.bfloat16),
        "gain_key": jnp.clip(1.0 + 0.15 * jax.random.normal(key_list[7], (D,), jnp.float32), 0.25, 1.75).astype(jnp.bfloat16),
        "gain_attn": jnp.clip(1.0 + 0.15 * jax.random.normal(key_list[8], (D,), jnp.float32), 0.25, 1.75).astype(jnp.bfloat16),
        "w_gate": normal_values(key_list[9], (D, FF), D ** -0.5, 0.125, ((0, 8),)),
        "w_up": normal_values(key_list[10], (D, FF), D ** -0.5, 0.125, ((0, 8),)),
        "w_down": normal_values(key_list[11], (FF, D), FF ** -0.5, 0.0625, ((0, 8),)),
        "gain_mlp": jnp.clip(1.0 + 0.15 * jax.random.normal(key_list[12], (D,), jnp.float32), 0.25, 1.75).astype(jnp.bfloat16),
        "out_cotangent": normal_values(key_list[13], (TOKENS, D), 1.0, 6.0, ((0, 32),)),
    }


@jax.custom_vjp
def low(v):
    return lax.optimization_barrier(v.astype(jnp.bfloat16)).astype(jnp.float32)

@jax.custom_vjp
def low_back(v):
    return v

def low_keep(v):
    return (low(v), None)

def low_pass(kept, grad):
    return (grad,)

def back_keep(v):
    return (v, None)

def back_low(kept, grad):
    return (low(grad),)
low.defvjp(low_keep, low_pass)
low_back.defvjp(back_keep, back_low)
EPS = 1e-06
THETA = 500000.0
NEG = -1e+30
HIGH = lax.Precision.HIGHEST

def matmul(left_rows, right_rows):
    return jnp.dot(left_rows, right_rows, precision=HIGH, preferred_element_type=jnp.float32)

def rms_norm(values, gain_vec):
    return values * lax.rsqrt(lax.optimization_barrier(jnp.mean(values * values, axis=-1, keepdims=True)) + EPS) * gain_vec

def rotate(values, cosine, sine_table):
    half_dim = values.shape[-1] // 2
    first_half = values[..., :half_dim]
    second = values[..., half_dim:]
    return jnp.concatenate([first_half * cosine - second * sine_table, second * cosine + first_half * sine_table], axis=-1)

def mask_tables(segments, head_dim):
    row_total = segments.shape[1]
    row_index = jnp.arange(row_total, dtype=jnp.int32)
    same_seg = segments[:, :, None] == segments[:, None, :]
    allowed = jnp.logical_and(same_seg, row_index[:, None] >= row_index[None, :])
    position = lax.optimization_barrier(jnp.sum(allowed.astype(jnp.int32), axis=2)) - 1
    half_dim = head_dim // 2
    frequency = THETA ** (-2.0 * jnp.arange(half_dim, dtype=jnp.float32) / head_dim)
    angles = position.astype(jnp.float32)[:, :, None, None] * frequency
    return (allowed, jnp.cos(angles), jnp.sin(angles))

def block_forward(x_rows, segments, weights):
    w_query, w_key, w_value, w_out, gain_query, gain_key, gain_attn, w_gate, w_up, w_down, gain_mlp = weights
    groups_here, block_rows = segments.shape
    allowed, cosine, sine_table = mask_tables(segments, HEAD_DIM)
    live_rows = (segments.reshape(-1) >= 0).astype(jnp.float32)[:, None]
    q_raw = low_back(matmul(x_rows, w_query))
    k_raw = low_back(matmul(x_rows, w_key))
    value_low = low_back(low(matmul(x_rows, w_value))).reshape(groups_here, block_rows, HEADS, HEAD_DIM)
    query = low(rotate(rms_norm(q_raw, gain_query).reshape(groups_here, block_rows, HEADS, HEAD_DIM), cosine, sine_table))
    key_rot = low(rotate(rms_norm(k_raw, gain_key).reshape(groups_here, block_rows, HEADS, HEAD_DIM), cosine, sine_table))
    scores = low_back(jnp.einsum('gqhd,gkhd->ghqk', query, key_rot, precision=HIGH) * HEAD_DIM ** (-0.5))
    scores = jnp.where(allowed[:, None], scores, NEG)
    probs = low(jax.nn.softmax(scores, axis=-1))
    attended = low_back(low(jnp.einsum('ghqk,gkhd->gqhd', probs, value_low, precision=HIGH))).reshape(-1, D)
    branch = low_back(matmul(attended, w_out))
    middle = x_rows + rms_norm(branch, gain_attn)
    middle_low = low(middle)
    gate = low_back(matmul(middle_low, w_gate))
    up_proj = low_back(matmul(middle_low, w_up))
    hidden = low(jax.nn.silu(gate) * up_proj)
    mixed = low_back(matmul(hidden, w_down))
    return (middle + rms_norm(mixed, gain_mlp)) * live_rows

def reference(block_input, segment_ids, w_query, w_key, w_value, w_out, gain_query, gain_key, gain_attn, w_gate, w_up, w_down, gain_mlp, out_cotangent):
    blocks = TOKENS // MB
    group_size = math.gcd(blocks, max(1, 4096 // MB))
    steps_count = blocks // group_size
    inputs = block_input.astype(jnp.float32).reshape(steps_count, group_size * MB, D)
    segments = segment_ids.reshape(steps_count, group_size, MB)
    weights = tuple((entry.astype(jnp.float32) for entry in (w_query, w_key, w_value, w_out, gain_query, gain_key, gain_attn, w_gate, w_up, w_down, gain_mlp)))
    checked = jax.checkpoint(block_forward)

    def forward(all_inputs, all_weights):

        def advance(carry, scan_item):
            return (carry, checked(scan_item[0], scan_item[1], all_weights))
        unused, result = lax.scan(advance, None, (all_inputs, segments))
        return result
    outputs, pull_back = jax.vjp(forward, inputs, weights)
    cotangent = out_cotangent.astype(jnp.float32).reshape(steps_count, group_size * MB, D)
    input_grad, weight_grads = pull_back(cotangent)
    return (outputs.reshape(TOKENS, D).astype(jnp.bfloat16), input_grad.reshape(TOKENS, D), weight_grads[0], weight_grads[1], weight_grads[2], weight_grads[3], weight_grads[4], weight_grads[5], weight_grads[6], weight_grads[7], weight_grads[8], weight_grads[9], weight_grads[10])
```

```python
import jax
import jax.numpy as jnp
from jax import lax
from jax.experimental import pallas as pl
from jax.experimental.pallas import tpu as pltpu
from jax.sharding import Mesh, PartitionSpec as P

D = 2048
HEADS = 16
HEAD_DIM = 128
MB = 128
EPS = 1e-06
THETA = 500000.0
NEG = -1e30
BF = jnp.bfloat16
F32 = jnp.float32
SWAP = [(0, 1), (1, 0)]
BLOCK = 256
PARTS = ((0, 2), (2, 4), (6, 2))
HALVES = (slice(0, D // 2), slice(D // 2, D))


def product(left_rows, right_rows):
    return jnp.dot(left_rows, right_rows, preferred_element_type=F32)


def product_nt(left_rows, right_rows):
    return lax.dot_general(left_rows, right_rows, (((1,), (1,)), ((), ())), preferred_element_type=F32)


def product_tn(left_rows, right_rows):
    return lax.dot_general(left_rows, right_rows, (((0,), (0,)), ((), ())), preferred_element_type=F32)


def swap(values, axis):
    return lax.ppermute(values, axis, SWAP)


def plane_gather(rows):
    half = rows.shape[0] // 2
    by_a = swap(rows, "a")
    by_y = swap(rows, "y")
    top = swap(by_y[:half], "a")
    bottom = swap(by_a[half:], "y")
    far_a, far_y, far_top, far_bottom = (swap(piece, "c") for piece in (by_a, by_y, top, bottom))
    return jnp.concatenate(
        [top, bottom, far_top, far_bottom, by_a, far_a, by_y, far_y, rows, swap(rows, "c")], axis=0
    )


def plane_gather_small(values):
    values = jnp.concatenate([values, swap(values, "c")], axis=0)
    for axis in ("y", "a"):
        values = jnp.concatenate([swap(values, axis), values], axis=0)
    return values


def resident(shape):
    return pl.BlockSpec(shape, lambda i: (0,) * len(shape), pipeline_mode=pl.Buffered(1))


def row_block(columns, first=0):
    return pl.BlockSpec((BLOCK, columns), lambda i: (first + i, 0))


def stat_block(first=0):
    return pl.BlockSpec((2, BLOCK), lambda i: (0, first + i))


def call(kernel, grid, in_specs, out_specs, out_shape, flops, args, after=(), **more):
    extra = len(after)
    known = len(args)
    moved = sum(v.size * v.dtype.itemsize for v in args)
    moved += sum(v.size * v.dtype.itemsize for v in jax.tree.leaves(out_shape))

    def body(*refs):
        kernel(*refs[:known], *refs[known + extra :])

    return pl.pallas_call(
        body,
        grid=grid,
        in_specs=list(in_specs) + [pl.BlockSpec(memory_space=pl.ANY)] * extra,
        out_specs=out_specs,
        out_shape=out_shape,
        compiler_params=pltpu.CompilerParams(vmem_limit_bytes=44 * 1024 * 1024),
        cost_estimate=pl.CostEstimate(flops=flops, bytes_accessed=moved, transcendentals=0),
        **more,
    )(*args, *after)


def eye():
    shape = (MB, MB)
    return lax.broadcasted_iota(jnp.int32, shape, 0) == lax.broadcasted_iota(jnp.int32, shape, 1)


def as_column(row):
    return jnp.sum(jnp.where(eye(), row, 0.0), axis=1, keepdims=True)


def as_row(column):
    return jnp.sum(jnp.where(eye(), column, 0.0), axis=0, keepdims=True)


def allowed_pairs(segment_row):
    shape = (MB, MB)
    earlier = lax.broadcasted_iota(jnp.int32, shape, 0) >= lax.broadcasted_iota(jnp.int32, shape, 1)
    return jnp.logical_and(as_column(segment_row) == segment_row, earlier)


def qkv_kernel(x_ref, w_ref, qkv_ref, squares_ref):
    width = w_ref.shape[1] // 3
    qkv = product(x_ref[...], w_ref[...])
    qkv_ref[...] = qkv
    for kind in range(2):
        part = qkv[:, kind * width : (kind + 1) * width]
        total = jnp.sum(part * part, axis=1, keepdims=True)
        for m in range(BLOCK // MB):
            squares_ref[kind : kind + 1, m * MB : (m + 1) * MB] = as_row(total[m * MB : (m + 1) * MB])


def attention_kernel(qkv_ref, squares_ref, seg_ref, cos_ref, sin_ref, gain_ref, out_ref, low_ref, att_ref, part_ref):
    width = gain_ref.shape[1]
    scales = lax.rsqrt(squares_ref[...] / D + EPS)
    for m in range(BLOCK // MB):
        rows = slice(m * MB, (m + 1) * MB)
        allowed = allowed_pairs(seg_ref[:, rows])
        cosine, sine = cos_ref[rows, :], sin_ref[rows, :]
        row_scale = [as_column(scales[kind : kind + 1, rows]) for kind in range(2)]
        for h in range(width // HEAD_DIM):
            cols = slice(h * HEAD_DIM, (h + 1) * HEAD_DIM)
            turned = []
            for kind in range(2):
                at = slice(kind * width + h * HEAD_DIM, kind * width + (h + 1) * HEAD_DIM)
                u = qkv_ref[rows, at] * row_scale[kind] * gain_ref[kind : kind + 1, cols]
                u = (u * cosine + pltpu.roll(u, HEAD_DIM // 2, 1) * sine).astype(BF)
                low_ref[rows, at] = u
                turned.append(u)
            at = slice(2 * width + h * HEAD_DIM, 2 * width + (h + 1) * HEAD_DIM)
            value = qkv_ref[rows, at].astype(BF)
            low_ref[rows, at] = value
            scores = jnp.where(allowed, product_nt(turned[0], turned[1]) * HEAD_DIM**-0.5, NEG)
            e = jnp.exp(scores - jnp.max(scores, axis=1, keepdims=True))
            probs = (e / jnp.sum(e, axis=1, keepdims=True)).astype(BF)
            att_ref[rows, cols] = product(probs, value).astype(BF)
    part_ref[...] = product(att_ref[...], out_ref[...]).astype(BF)


def attention_back_kernel(
    low_ref, qkv_ref, squares_ref, seg_ref, cos_ref, sin_ref, gain_ref, out_ref, db_ref,
    n_ref, dv_ref, dots_ref, gain_part_ref,
):
    width = gain_ref.shape[1]
    scales = lax.rsqrt(squares_ref[...] / D + EPS)
    d_att = product_nt(db_ref[...], out_ref[...]).astype(BF)
    terms = [[jnp.zeros((1, HEAD_DIM), F32) for _ in range(width // HEAD_DIM)] for _ in range(2)]
    for m in range(BLOCK // MB):
        rows = slice(m * MB, (m + 1) * MB)
        allowed = allowed_pairs(seg_ref[:, rows])
        cosine, sine = cos_ref[rows, :], sin_ref[rows, :]
        dots = [jnp.zeros((MB, 1), F32), jnp.zeros((MB, 1), F32)]
        for h in range(width // HEAD_DIM):
            cols = slice(h * HEAD_DIM, (h + 1) * HEAD_DIM)
            query, key, value = (
                low_ref[rows, kind * width + h * HEAD_DIM : kind * width + (h + 1) * HEAD_DIM] for kind in range(3)
            )
            scores = jnp.where(allowed, product_nt(query, key) * HEAD_DIM**-0.5, NEG)
            e = jnp.exp(scores - jnp.max(scores, axis=1, keepdims=True))
            probs = e / jnp.sum(e, axis=1, keepdims=True)
            d_out = d_att[rows, cols]
            d_probs = product_nt(d_out, value)
            dv_ref[rows, cols] = product_tn(probs.astype(BF), d_out).astype(BF)
            inner = jnp.sum(probs * d_probs, axis=1, keepdims=True)
            d_scores = (probs * (d_probs - inner)).astype(BF)
            grads = (product(d_scores, key), product_tn(d_scores, query))
            for kind in range(2):
                at = slice(kind * width + h * HEAD_DIM, kind * width + (h + 1) * HEAD_DIM)
                u = grads[kind] * HEAD_DIM**-0.5
                u = u * cosine - pltpu.roll(u, HEAD_DIM // 2, 1) * sine
                raw = qkv_ref[rows, at]
                n = u * gain_ref[kind : kind + 1, cols]
                n_ref[rows, at] = n
                dots[kind] += jnp.sum(n * raw, axis=1, keepdims=True)
                scaled = raw * as_column(scales[kind : kind + 1, rows])
                terms[kind][h] += jnp.sum(u * scaled, axis=0, keepdims=True)
        for kind in range(2):
            dots_ref[kind : kind + 1, rows] = as_row(dots[kind])
    for kind in range(2):
        for h in range(width // HEAD_DIM):
            gain_part_ref[0, kind : kind + 1, h * HEAD_DIM : (h + 1) * HEAD_DIM] = terms[kind][h]


def qkv_back_kernel(n_ref, qkv_ref, squares_ref, dots_ref, dv_ref, out_ref):
    width = dv_ref.shape[1]
    scales = lax.rsqrt(squares_ref[...] / D + EPS)
    factors = scales * scales * scales * dots_ref[...] / D
    for m in range(BLOCK // MB):
        rows = slice(m * MB, (m + 1) * MB)
        for kind in range(2):
            at = slice(kind * width, (kind + 1) * width)
            near = as_column(scales[kind : kind + 1, rows])
            far = as_column(factors[kind : kind + 1, rows])
            out_ref[rows, at] = (near * n_ref[rows, at] - far * qkv_ref[rows, at]).astype(BF)
    out_ref[:, 2 * width :] = dv_ref[...]


def gate_up_kernel(mid_ref, w_ref, gate_up_ref, hidden_ref):
    half = hidden_ref.shape[1]
    both = product(mid_ref[...], w_ref[...])
    gate, up = both[:, :half], both[:, half:]
    gate_up_ref[...] = both.astype(BF)
    hidden_ref[...] = (gate / (1.0 + jnp.exp(-gate)) * up).astype(BF)


def hidden_back_kernel(dm0_ref, dm1_ref, w0_ref, w1_ref, gate_up_ref, out_ref):
    half = w0_ref.shape[0]
    d_hidden = product_nt(dm0_ref[...], w0_ref[...]) + product_nt(dm1_ref[...], w1_ref[...])
    gate = gate_up_ref[:, :half].astype(F32)
    up = gate_up_ref[:, half:].astype(F32)
    sig = 1.0 / (1.0 + jnp.exp(-gate))
    out_ref[:, :half] = (d_hidden * up * sig * (1.0 + gate * (1.0 - sig))).astype(BF)
    out_ref[:, half:] = (d_hidden * gate * sig).astype(BF)


def block_product(left, right, first, count, transposed=False, after=()):
    columns = right.shape[0] if transposed else right.shape[1]

    def kernel(left_ref, right_ref, out_ref):
        out_ref[...] = (product_nt if transposed else product)(left_ref[...], right_ref[...]).astype(BF)

    return call(
        kernel, (count,), [row_block(left.shape[1], first), resident(right.shape)], row_block(columns),
        jax.ShapeDtypeStruct((count * BLOCK, columns), BF), 2 * count * BLOCK * left.shape[1] * columns,
        (left, right), after,
    )


def plane_product(left, right, transposed=False, after=()):
    return tuple(block_product(left, right, first, count, transposed, after) for first, count in PARTS)


def assemble(pieces, out_shape, rows, columns, steps, spots, place, scalars):
    count = len(pieces)
    outs = len(out_shape)

    def in_map(k, o):
        def index(j, s, scalars):
            at = spots(o, jnp.where(j == k, s, jnp.where(j < k, 0, steps - 1)))
            return at

        return index

    def out_map(o):
        return lambda j, s, scalars: place(o, j, s, scalars)

    def kernel(scalar_ref, *refs):
        j = pl.program_id(0)
        for k in range(count):

            @pl.when(j == k)
            def _():
                for o in range(outs):
                    refs[count * outs + o][...] = refs[k * outs + o][...].astype(F32)

    moved = sum(6 * p.size for p in pieces)
    return pl.pallas_call(
        kernel,
        grid_spec=pltpu.PrefetchScalarGridSpec(
            num_scalar_prefetch=1,
            grid=(count, steps),
            in_specs=[pl.BlockSpec((rows, columns), in_map(k, o)) for k in range(count) for o in range(outs)],
            out_specs=[pl.BlockSpec((rows, columns), out_map(o)) for o in range(outs)],
        ),
        out_shape=out_shape,
        compiler_params=pltpu.CompilerParams(vmem_limit_bytes=44 * 1024 * 1024),
        cost_estimate=pl.CostEstimate(flops=0, bytes_accessed=moved, transcendentals=0),
    )(scalars, *[p for p in pieces for _ in range(outs)])


def plane_scatter(parts):
    corner_part, next_part, own_part = parts
    rows = own_part.shape[0] // 2
    half = rows // 2
    corner = (corner_part[:rows].astype(F32) + swap(corner_part[rows:], "c").astype(F32)).astype(BF)
    from_a = swap(corner[:half], "a").astype(F32)
    from_y = swap(corner[half:], "y").astype(F32)
    a_near = next_part[:rows].astype(F32) + swap(next_part[rows : 2 * rows], "c").astype(F32)
    y_near = next_part[2 * rows : 3 * rows].astype(F32) + swap(next_part[3 * rows :], "c").astype(F32)
    to_a = jnp.concatenate([a_near[:half], a_near[half:] + from_y], axis=0).astype(BF)
    to_y = jnp.concatenate([y_near[:half] + from_a, y_near[half:]], axis=0).astype(BF)
    own = own_part[:rows].astype(F32) + swap(own_part[rows:], "c").astype(F32)
    return own + swap(to_a, "a").astype(F32) + swap(to_y, "y").astype(F32)


def plane_sum_tokens(stats):
    kinds, _, count = stats.shape
    values = stats.reshape(kinds, 2, 2, 2, count)
    for axis, dim in (("a", 1), ("y", 2), ("c", 3)):
        values = values + jnp.flip(swap(values, axis), dim)
    return values.reshape(kinds, 8, count)


def sum_everywhere(values, planes):
    for axis in ("a", "c", "y"):
        values = values + swap(values, axis)
    step = 1
    while step < planes:
        values = values + lax.ppermute(values, "z", [(i, i ^ step) for i in range(planes)])
        step *= 2
    return values


def gather_owners(values, planes):
    z = lax.axis_index("z")
    values = ordered_pair(values, swap(values, "y"), lax.axis_index("y"))
    step = 1
    while step < planes:
        other = lax.ppermute(values, "z", [(i, i ^ step) for i in range(planes)])
        pair = ordered_pair(values, other, (z // step) % 2)
        values = pair.reshape((-1,) + pair.shape[2:])
        step *= 2
    return values


def spread(pieces):
    both = list(pieces) + [swap(piece, "a") for piece in pieces]
    return both + [swap(piece, "c") for piece in both]


def ordered_pair(mine, other, index, axis=0):
    return jnp.where(index == 0, jnp.stack([mine, other], axis=axis), jnp.stack([other, mine], axis=axis))


def rotation_tables(segments):
    row_index = jnp.arange(MB, dtype=jnp.int32)
    same_seg = segments[:, :, None] == segments[:, None, :]
    allowed = jnp.logical_and(same_seg, row_index[:, None] >= row_index[None, :])
    position = jnp.sum(allowed.astype(jnp.int32), axis=2) - 1
    half_dim = HEAD_DIM // 2
    frequency = THETA ** (-2.0 * jnp.arange(half_dim, dtype=F32) / HEAD_DIM)
    angles = position.astype(F32).reshape(-1, 1) * frequency
    cosine, sine = jnp.cos(angles), jnp.sin(angles)
    return jnp.concatenate([cosine, cosine], axis=1), jnp.concatenate([-sine, sine], axis=1)


def make_body(planes):
    def body(
        block_input, segment_ids, w_query, w_key, w_value, w_out, gain_query, gain_key, gain_attn,
        w_gate, w_up, w_down, gain_mlp, out_cotangent,
    ):
        a = lax.axis_index("a")
        c = lax.axis_index("c")
        z = lax.axis_index("z")
        y = lax.axis_index("y")
        member = a * 2 + c
        pair = member * 2 + y
        own_rows = block_input.shape[0]
        all_rows = own_rows * 8
        shard_rows = w_query.shape[0]
        width = D // 8
        ff_shard = w_down.shape[0]
        quarter = ff_shard // 4
        ff_here = planes * quarter
        blocks = all_rows // BLOCK

        gains = gather_owners(jnp.stack([gain_query, gain_key, gain_attn, gain_mlp]).astype(F32), planes)
        gains = jnp.transpose(gains, (1, 0, 2)).reshape(4, D)
        gain_q = lax.dynamic_slice(gains[0], (pair * width,), (width,))
        gain_k = lax.dynamic_slice(gains[1], (pair * width,), (width,))
        gain_a, gain_m = gains[2], gains[3]
        segments = plane_gather_small(segment_ids.reshape(own_rows // MB, MB))
        live = (segment_ids >= 0).astype(F32)[:, None]

        def columns_of(which_y):
            at = (member * 2 + which_y) * width
            return jnp.concatenate(
                [lax.dynamic_slice(w, (0, at), (shard_rows, width)) for w in (w_query, w_key, w_value)], axis=1
            )

        def hidden_columns_of(which_y):
            starts = [((plane * 2 + which_y) * 4 + member) * quarter for plane in range(planes)]
            return jnp.concatenate(
                [lax.dynamic_slice(w, (0, at), (shard_rows, quarter)) for w in (w_gate, w_up) for at in starts], axis=1
            )

        def column_weights(mine, given):
            both = ordered_pair(mine, swap(given, "y"), y)
            return lax.all_gather(both.reshape(2 * shard_rows, -1), "z", axis=0, tiled=True)

        if planes == 4:
            out_piece = lax.dynamic_slice(w_out, (member * (shard_rows // 4), 0), (shard_rows // 4, D))
            out_pieces = lax.all_gather(out_piece, "z", axis=0, tiled=True)
            out_rows = lax.all_to_all(out_pieces, ("a", "c"), split_axis=0, concat_axis=0, tiled=True)
        else:
            out_rows = lax.dynamic_slice(
                lax.all_gather(w_out, ("z", "y"), axis=0, tiled=True), (pair * width, 0), (width, D)
            )
        qkv_w = column_weights(columns_of(y), columns_of(1 - y))
        gu_w = column_weights(hidden_columns_of(y), hidden_columns_of(1 - y))
        down_piece = lax.dynamic_slice(w_down, (member * quarter, 0), (quarter, D))
        down_w = [lax.all_gather(down_piece[:, cut], "z", axis=0, tiled=True) for cut in HALVES]

        x_all = plane_gather(block_input)
        shaped = jax.ShapeDtypeStruct
        qkv, squares = call(
            qkv_kernel, (blocks,), [row_block(D), resident((D, 3 * width))], [row_block(3 * width), stat_block()],
            [shaped((all_rows, 3 * width), F32), shaped((2, all_rows), F32)], 2 * all_rows * D * 3 * width,
            (x_all, qkv_w),
        )
        squares = plane_sum_tokens(squares.reshape(2, 8, own_rows)).reshape(2, all_rows)
        cosine, sine = rotation_tables(segments)
        seg_row = segments.astype(F32).reshape(1, all_rows)
        gain_qk = jnp.stack([gain_q, gain_k])

        def attention(first, count):
            return call(
                attention_kernel, (count,),
                [
                    row_block(3 * width, first), stat_block(first), pl.BlockSpec((1, BLOCK), lambda i: (0, first + i)),
                    row_block(HEAD_DIM, first), row_block(HEAD_DIM, first), resident((2, width)), resident((width, D)),
                ],
                [row_block(3 * width), row_block(width), row_block(D)],
                [shaped((count * BLOCK, cols), BF) for cols in (3 * width, width, D)],
                2 * count * BLOCK * width * (D + 2 * MB),
                (qkv, squares, seg_row, cosine, sine, gain_qk, out_rows),
            )

        lows, atts, branch_parts = zip(*[attention(first, count) for first, count in PARTS])
        attended = jnp.concatenate(atts, axis=0)
        low = jnp.concatenate(lows, axis=0)
        branch = plane_scatter(branch_parts)

        def row_scale(values):
            return lax.rsqrt(jnp.mean(values * values, axis=-1, keepdims=True) + EPS)

        def norm_back(values, scale_here, gain, upstream):
            n = upstream * gain
            grad = scale_here * n - scale_here**3 * values * jnp.mean(n * values, axis=-1, keepdims=True)
            return grad, jnp.sum(upstream * values * scale_here, axis=0)

        branch_scale = row_scale(branch)
        middle = block_input.astype(F32) + branch * branch_scale * gain_a
        mid_all = plane_gather(middle.astype(BF))

        gate_up, hidden = call(
            gate_up_kernel, (blocks,), [row_block(D), resident((D, 2 * ff_here))],
            [row_block(2 * ff_here), row_block(ff_here)],
            [shaped((all_rows, 2 * ff_here), BF), shaped((all_rows, ff_here), BF)], 4 * all_rows * D * ff_here,
            (mid_all, gu_w),
        )
        mixed0 = plane_scatter(plane_product(hidden, down_w[0]))
        mixed1 = plane_scatter(plane_product(hidden, down_w[1], after=(mixed0,)))
        mixed = jnp.concatenate([mixed0, mixed1], axis=1)
        mixed_scale = row_scale(mixed)
        block_output = ((middle + mixed * mixed_scale * gain_m) * live).astype(BF)

        grad_rows = out_cotangent.astype(F32) * live
        d_mixed, d_gain_mlp = norm_back(mixed, mixed_scale, gain_m, grad_rows)
        dm_all = [plane_gather(d_mixed[:, cut].astype(BF)) for cut in HALVES]

        def plane_sum(values):
            return lax.psum_scatter(values.astype(BF), "z", scatter_dimension=0, tiled=True)

        grad_down_parts = [product_tn(hidden, cut).astype(BF) for cut in dm_all]
        grad_down = [plane_sum(part) for part in grad_down_parts]
        d_gu = call(
            hidden_back_kernel, (blocks,),
            [row_block(D // 2), row_block(D // 2), resident((ff_here, D // 2)), resident((ff_here, D // 2)),
             row_block(2 * ff_here)],
            row_block(2 * ff_here), shaped((all_rows, 2 * ff_here), BF), 2 * all_rows * D * ff_here,
            (*dm_all, *down_w, gate_up), grad_down_parts,
        )
        grad_gu = plane_sum(product_tn(mid_all, d_gu))
        d_middle = grad_rows + plane_scatter(plane_product(d_gu, gu_w, True))

        d_branch, d_gain_attn = norm_back(branch, branch_scale, gain_a, d_middle)
        db_all = plane_gather(d_branch.astype(BF))
        grad_out = product_tn(attended, db_all).astype(BF)
        n_qk, d_value, dots, gain_part = call(
            attention_back_kernel, (blocks,),
            [
                row_block(3 * width), row_block(2 * width), stat_block(), pl.BlockSpec((1, BLOCK), lambda i: (0, i)),
                row_block(HEAD_DIM), row_block(HEAD_DIM), resident((2, width)), resident((width, D)), row_block(D),
            ],
            [row_block(2 * width), row_block(width), stat_block(), pl.BlockSpec((1, 2, width), lambda i: (i, 0, 0))],
            [
                shaped((all_rows, 2 * width), F32), shaped((all_rows, width), BF), shaped((2, all_rows), F32),
                shaped((blocks, 2, width), F32),
            ],
            2 * all_rows * width * (D + 5 * MB),
            (low, qkv, squares, seg_row, cosine, sine, gain_qk, out_rows, db_all),
        )
        d_gain_query, d_gain_key = jnp.sum(gain_part, axis=0)
        dots = plane_sum_tokens(dots.reshape(2, 8, own_rows)).reshape(2, all_rows)
        d_qkv = call(
            qkv_back_kernel, (blocks,),
            [row_block(2 * width), row_block(2 * width), stat_block(), stat_block(), row_block(width)],
            row_block(3 * width), shaped((all_rows, 3 * width), BF), 0, (n_qk, qkv, squares, dots, d_value),
        )
        grad_qkv_part = product_tn(x_all, d_qkv).astype(BF)
        grad_qkv = plane_sum(grad_qkv_part)
        d_input = d_middle + plane_scatter(plane_product(d_qkv, qkv_w, True, after=(grad_qkv_part,)))

        scalars = jnp.stack([a, c, y]).astype(jnp.int32)

        def member_of(j_a, j_c, scalars):
            return (scalars[0] ^ j_a) * 2 + (scalars[1] ^ j_c)

        down_pieces = [piece for pair_ in zip(*[spread([cut]) for cut in grad_down]) for piece in pair_]
        (grad_down,) = assemble(
            down_pieces, [shaped((ff_shard, D), F32)], quarter, D // 2, 1, lambda o, s: (0, 0),
            lambda o, j, s, scalars: (member_of((j // 2) % 2, j // 4, scalars), j % 2), scalars,
        )

        def column_pieces(summed):
            split = summed.reshape(2, shard_rows, -1)
            mine = lax.dynamic_index_in_dim(split, y, 0, keepdims=False)
            given = lax.dynamic_index_in_dim(split, 1 - y, 0, keepdims=False)
            return spread([mine, swap(given, "y")])

        def column_pair(j, scalars):
            return member_of((j // 2) % 2, j // 4, scalars), scalars[2] ^ (j % 2)

        def gu_place(o, j, s, scalars):
            owner, which_y = column_pair(j, scalars)
            return 0, (s * 2 + which_y) * 4 + owner

        gu_pieces = column_pieces(grad_gu)
        if quarter % 128 == 0:
            grad_gate, grad_up = assemble(
                gu_pieces, [shaped((shard_rows, 8 * ff_here), F32)] * 2, shard_rows, quarter, planes,
                lambda o, s: (0, o * planes + s), gu_place, scalars,
            )
        else:
            filled = jnp.zeros((shard_rows, 2, planes, 2, 4, quarter), F32)
            for j, piece in enumerate(gu_pieces):
                owner, which_y = column_pair(j, scalars)
                piece = piece.astype(F32).reshape(shard_rows, 2, planes, 1, 1, quarter)
                filled = lax.dynamic_update_slice(filled, piece, (0, 0, 0, which_y, owner, 0))
            grad_gate, grad_up = (filled[:, o].reshape(shard_rows, 8 * ff_here) for o in range(2))

        def qkv_place(o, j, s, scalars):
            owner, which_y = column_pair(j, scalars)
            return 0, owner * 2 + which_y

        grad_query, grad_key, grad_value = assemble(
            column_pieces(grad_qkv), [shaped((shard_rows, D), F32)] * 3, shard_rows, width, 1,
            lambda o, s: (0, o), qkv_place, scalars,
        )
        if planes == 4:
            grad_out = lax.all_to_all(grad_out, ("a", "c"), split_axis=0, concat_axis=0, tiled=True)
            (grad_out,) = assemble(
                spread([plane_sum(grad_out)]), [shaped((shard_rows, D), F32)], shard_rows // 4, D, 1,
                lambda o, s: (0, 0), lambda o, j, s, scalars: (member_of(j % 2, j // 2, scalars), 0), scalars,
            )
        else:
            whole = lax.dynamic_update_slice(jnp.zeros((D, D), BF), grad_out, (pair * width, 0))
            whole = lax.psum_scatter(whole, ("z", "y"), scatter_dimension=0, tiled=True)
            grad_out = lax.psum(whole, ("a", "c")).astype(F32)

        zero = jnp.zeros((D,), F32)
        gain_terms = jnp.stack(
            [
                lax.dynamic_update_slice(zero, d_gain_query, (pair * width,)),
                lax.dynamic_update_slice(zero, d_gain_key, (pair * width,)),
                d_gain_attn,
                d_gain_mlp,
            ]
        )
        gain_terms = sum_everywhere(gain_terms, planes)
        own_gains = lax.dynamic_slice(gain_terms, (0, (z * 2 + y) * shard_rows), (4, shard_rows))
        return (
            block_output,
            d_input,
            grad_query,
            grad_key,
            grad_value,
            grad_out,
            own_gains[0],
            own_gains[1],
            own_gains[2],
            grad_gate,
            grad_up,
            grad_down,
            own_gains[3],
        )

    return body


def solution(mesh):
    replicas, shards = mesh.shape["dp"], mesh.shape["fsdp"]
    planes = shards // 2
    fine = Mesh(mesh.devices.reshape(replicas // 2, 2, planes, 2), ("a", "c", "z", "y"))
    tokens = ("a", "c", "z", "y")
    owner = ("z", "y")
    rows, row, wide, vec = P(tokens, None), P(tokens), P(owner, None), P(owner)
    in_specs = (rows, row, wide, wide, wide, wide, vec, vec, vec, wide, wide, wide, vec, rows)
    out_specs = (rows, rows, wide, wide, wide, wide, vec, vec, vec, wide, wide, wide, vec)
    return jax.shard_map(make_body(planes), mesh=fine, in_specs=in_specs, out_specs=out_specs, check_vma=False)
```

```python
import jax
import jax.numpy as jnp
from jax import lax
from jax.experimental import pallas as pl
from jax.experimental.pallas import tpu as pltpu
from jax.sharding import Mesh, PartitionSpec as P

D = 2048
HEADS = 16
HEAD_DIM = 128
MB = 128
EPS = 1e-06
THETA = 500000.0
NEG = -1e30
BF = jnp.bfloat16
F32 = jnp.float32
SWAP = [(0, 1), (1, 0)]
BLOCK = 256
PARTS = ((0, 2), (2, 4), (6, 2))
VMEM_LIMIT = 40 * 1024 * 1024


def cost(flops, *arrays):
    moved = sum(v.size * v.dtype.itemsize for v in arrays)
    return pl.CostEstimate(flops=flops, bytes_accessed=moved, transcendentals=0)
HALVES = (slice(0, D // 2), slice(D // 2, D))


def product(left_rows, right_rows):
    return jnp.dot(left_rows, right_rows, preferred_element_type=F32)


def product_nt(left_rows, right_rows):
    return lax.dot_general(left_rows, right_rows, (((1,), (1,)), ((), ())), preferred_element_type=F32)


def product_tn(left_rows, right_rows):
    return lax.dot_general(left_rows, right_rows, (((0,), (0,)), ((), ())), preferred_element_type=F32)


def swap(values, axis):
    return lax.ppermute(values, axis, SWAP)


def plane_gather(rows, early=None, hold=()):
    half = rows.shape[0] // 2
    by_a = swap(rows, "a")
    by_y = swap(rows, "y")
    if early is not None:
        early.extend((by_a, by_y))
    top, bottom = by_y[:half], by_a[half:]
    if hold:
        top, bottom = ordered(top, hold), ordered(bottom, hold)
    top = swap(top, "a")
    bottom = swap(bottom, "y")
    far_a, far_y, far_top, far_bottom = (swap(piece, "c") for piece in (by_a, by_y, top, bottom))
    pieces = [top, bottom, far_top, far_bottom, by_a, far_a, by_y, far_y, rows, swap(rows, "c")]
    return jnp.concatenate(pieces, axis=0)


def plane_gather_small(values):
    values = jnp.concatenate([values, swap(values, "c")], axis=0)
    for axis in ("y", "a"):
        values = jnp.concatenate([swap(values, axis), values], axis=0)
    return values


def assemble_hidden(pieces, columns, places, quarter, planes):
    rows, width = pieces[0].shape
    count = len(pieces)
    parts = 2 * planes

    def kernel(places_ref, *refs):
        ins, outs, held, sems = refs[:count], refs[count : count + 2], refs[count + 2], refs[count + 3]

        def copies(k):
            for n in range(parts):
                at = pl.multiple_of(places_ref[k, n % planes] * quarter, quarter)
                yield pltpu.make_async_copy(
                    held.at[k % 2, :, n * quarter : (n + 1) * quarter],
                    outs[n // planes].at[:, pl.ds(at, quarter)],
                    sems.at[k % 2, n],
                )

        for k in range(count):
            if k >= 2:
                for copy in copies(k - 2):
                    copy.wait()
            held[k % 2] = ins[k][...].astype(F32)
            for copy in copies(k):
                copy.start()
        for k in range(count - 2, count):
            for copy in copies(k):
                copy.wait()

    return pl.pallas_call(
        kernel,
        grid_spec=pltpu.PrefetchScalarGridSpec(
            num_scalar_prefetch=1,
            grid=(1,),
            in_specs=[pl.BlockSpec((rows, width), lambda i, s: (0, 0), pipeline_mode=pl.Buffered(1))] * count,
            out_specs=[pl.BlockSpec(memory_space=pl.ANY)] * 2,
            scratch_shapes=[pltpu.VMEM((2, rows, width), F32), pltpu.SemaphoreType.DMA((2, parts))],
        ),
        out_shape=[jax.ShapeDtypeStruct((rows, columns), F32)] * 2,
        compiler_params=pltpu.CompilerParams(vmem_limit_bytes=VMEM_LIMIT),
        cost_estimate=cost(0, *pieces, *pieces, *pieces),
    )(places, *pieces)


def resident(shape):
    return pl.BlockSpec(shape, lambda i: (0,) * len(shape), pipeline_mode=pl.Buffered(1))


def resident_view(view):
    array, rows, columns = view
    return resident((array.shape[0], rows, columns))


def flat(ref):
    value = ref[...]
    return value.reshape(-1, value.shape[-1]) if value.ndim == 3 else value


def row_block(columns, first=0):
    return pl.BlockSpec((BLOCK, columns), lambda i: (first + i, 0))


def stat_block(first=0):
    return pl.BlockSpec((2, BLOCK), lambda i: (0, first + i))


def call(kernel, grid, in_specs, out_specs, out_shape, flops, args, after=(), through=()):
    outs = isinstance(out_shape, (list, tuple))
    out_shape = list(out_shape) if outs else [out_shape]
    out_specs = list(out_specs) if outs else [out_specs]
    extra = len(after) + len(through)
    known = len(args)
    results = len(out_shape)

    def body(*refs):
        kernel(*refs[:known], *refs[known + extra : known + extra + results])

    anywhere = pl.BlockSpec(memory_space=pl.ANY)
    given = pl.pallas_call(
        body,
        grid=grid,
        in_specs=list(in_specs) + [anywhere] * extra,
        out_specs=out_specs + [anywhere] * len(through),
        out_shape=out_shape + [jax.ShapeDtypeStruct(v.shape, v.dtype) for v in through],
        input_output_aliases={known + len(after) + k: results + k for k in range(len(through))},
        compiler_params=pltpu.CompilerParams(vmem_limit_bytes=VMEM_LIMIT),
        cost_estimate=cost(flops, *args, *out_shape),
    )(*args, *after, *through)
    own = given[:results] if outs else given[0]
    return (own, *given[results:]) if through else own


def eye():
    shape = (MB, MB)
    return lax.broadcasted_iota(jnp.int32, shape, 0) == lax.broadcasted_iota(jnp.int32, shape, 1)


def as_column(row):
    return jnp.sum(jnp.where(eye(), row, 0.0), axis=1, keepdims=True)


def as_row(column):
    return jnp.sum(jnp.where(eye(), column, 0.0), axis=0, keepdims=True)


def allowed_pairs(segment_row):
    shape = (MB, MB)
    earlier = lax.broadcasted_iota(jnp.int32, shape, 0) >= lax.broadcasted_iota(jnp.int32, shape, 1)
    return jnp.logical_and(as_column(segment_row) == segment_row, earlier)


def qkv_kernel(x_ref, w_ref, qkv_ref, squares_ref):
    width = w_ref.shape[2] // 3
    qkv = product(x_ref[...], flat(w_ref))
    qkv_ref[...] = qkv
    for kind in range(2):
        part = qkv[:, kind * width : (kind + 1) * width]
        total = jnp.sum(part * part, axis=1, keepdims=True)
        for m in range(BLOCK // MB):
            squares_ref[kind : kind + 1, m * MB : (m + 1) * MB] = as_row(total[m * MB : (m + 1) * MB])


def head_slots(width):
    for m in range(BLOCK // MB):
        for h in range(width // HEAD_DIM):
            starts = [kind * width + h * HEAD_DIM for kind in range(3)]
            yield m, h, slice(m * MB, (m + 1) * MB), [slice(at, at + HEAD_DIM) for at in starts]


def masked_softmax(queries, keys, allowed):
    scores = [product_nt(query, key) * HEAD_DIM**-0.5 for query, key in zip(queries, keys)]
    scores = [jnp.where(mask, score, NEG) for mask, score in zip(allowed, scores)]
    tops = [jnp.max(score, axis=1, keepdims=True) for score in scores]
    powers = [jnp.exp(score - top) for score, top in zip(scores, tops)]
    sums = [jnp.sum(power, axis=1, keepdims=True) for power in powers]
    return [power / total for power, total in zip(powers, sums)]


def attention_kernel(qkv_ref, squares_ref, seg_ref, cos_ref, sin_ref, gain_ref, out_ref, low_ref, att_ref, part_ref):
    width = gain_ref.shape[1]
    scales = lax.rsqrt(squares_ref[...] / D + EPS)
    slots = list(head_slots(width))
    masks, columns = [], []
    for m in range(BLOCK // MB):
        rows = slice(m * MB, (m + 1) * MB)
        masks.append(allowed_pairs(seg_ref[:, rows]))
        columns.append([as_column(scales[kind : kind + 1, rows]) for kind in range(2)])
    lows = [[], [], []]
    for kind in range(2):
        for m, h, rows, ats in slots:
            gain = gain_ref[kind : kind + 1, h * HEAD_DIM : (h + 1) * HEAD_DIM]
            u = qkv_ref[rows, ats[kind]] * columns[m][kind] * gain
            lows[kind].append((u * cos_ref[rows, :] + pltpu.roll(u, HEAD_DIM // 2, 1) * sin_ref[rows, :]).astype(BF))
    lows[2] = [qkv_ref[rows, ats[2]].astype(BF) for m, h, rows, ats in slots]
    probs = masked_softmax(lows[0], lows[1], [masks[m] for m, *_ in slots])
    outs = [product(prob.astype(BF), value).astype(BF) for prob, value in zip(probs, lows[2])]
    for n, (m, h, rows, ats) in enumerate(slots):
        for kind in range(3):
            low_ref[rows, ats[kind]] = lows[kind][n]
        att_ref[rows, h * HEAD_DIM : (h + 1) * HEAD_DIM] = outs[n]
    part_ref[...] = product(att_ref[...], out_ref[...]).astype(BF)


def attention_back_kernel(
    low_ref, qkv_ref, squares_ref, seg_ref, cos_ref, sin_ref, gain_ref, out_ref, db_ref,
    n_ref, dv_ref, dots_ref, gain_part_ref,
):
    width = gain_ref.shape[1]
    scales = lax.rsqrt(squares_ref[...] / D + EPS)
    slots = list(head_slots(width))
    masks, columns = [], []
    for m in range(BLOCK // MB):
        rows = slice(m * MB, (m + 1) * MB)
        masks.append(allowed_pairs(seg_ref[:, rows]))
        columns.append([as_column(scales[kind : kind + 1, rows]) for kind in range(2)])
    queries, keys, values = ([low_ref[rows, ats[kind]] for m, h, rows, ats in slots] for kind in range(3))
    d_att = product_nt(db_ref[...], out_ref[...]).astype(BF)
    d_outs = [d_att[rows, h * HEAD_DIM : (h + 1) * HEAD_DIM] for m, h, rows, ats in slots]
    d_probs = [product_nt(d_out, value) for d_out, value in zip(d_outs, values)]
    probs = masked_softmax(queries, keys, [masks[m] for m, *_ in slots])
    d_values = [product_tn(prob.astype(BF), d_out).astype(BF) for prob, d_out in zip(probs, d_outs)]
    inner = [jnp.sum(prob * d_prob, axis=1, keepdims=True) for prob, d_prob in zip(probs, d_probs)]
    d_scores = [(prob * (d_prob - dot)).astype(BF) for prob, d_prob, dot in zip(probs, d_probs, inner)]
    grads = [
        [product(score, key) for score, key in zip(d_scores, keys)],
        [product_tn(score, query) for score, query in zip(d_scores, queries)],
    ]
    dots = [[jnp.zeros((MB, 1), F32) for _ in range(2)] for _ in range(BLOCK // MB)]
    terms = [[jnp.zeros((1, HEAD_DIM), F32) for _ in range(width // HEAD_DIM)] for _ in range(2)]
    for kind in range(2):
        for n, (m, h, rows, ats) in enumerate(slots):
            u = grads[kind][n] * HEAD_DIM**-0.5
            u = u * cos_ref[rows, :] - pltpu.roll(u, HEAD_DIM // 2, 1) * sin_ref[rows, :]
            raw = qkv_ref[rows, ats[kind]]
            grad = u * gain_ref[kind : kind + 1, h * HEAD_DIM : (h + 1) * HEAD_DIM]
            n_ref[rows, ats[kind]] = grad
            dots[m][kind] += jnp.sum(grad * raw, axis=1, keepdims=True)
            terms[kind][h] += jnp.sum(u * (raw * columns[m][kind]), axis=0, keepdims=True)
    for n, (m, h, rows, ats) in enumerate(slots):
        dv_ref[rows, h * HEAD_DIM : (h + 1) * HEAD_DIM] = d_values[n]
    for kind in range(2):
        for m in range(BLOCK // MB):
            dots_ref[kind : kind + 1, m * MB : (m + 1) * MB] = as_row(dots[m][kind])
        for h in range(width // HEAD_DIM):
            gain_part_ref[0, kind : kind + 1, h * HEAD_DIM : (h + 1) * HEAD_DIM] = terms[kind][h]


def qkv_back_kernel(n_ref, qkv_ref, squares_ref, dots_ref, dv_ref, out_ref):
    width = dv_ref.shape[1]
    scales = lax.rsqrt(squares_ref[...] / D + EPS)
    factors = scales * scales * scales * dots_ref[...] / D
    for m in range(BLOCK // MB):
        rows = slice(m * MB, (m + 1) * MB)
        for kind in range(2):
            at = slice(kind * width, (kind + 1) * width)
            near = as_column(scales[kind : kind + 1, rows])
            far = as_column(factors[kind : kind + 1, rows])
            out_ref[rows, at] = (near * n_ref[rows, at] - far * qkv_ref[rows, at]).astype(BF)
    out_ref[:, 2 * width :] = dv_ref[...]


def gate_up_kernel(mid_ref, w_ref, gate_up_ref, hidden_ref):
    half = hidden_ref.shape[1]
    both = product(mid_ref[...], flat(w_ref))
    gate, up = both[:, :half], both[:, half:]
    gate_up_ref[...] = both.astype(BF)
    hidden_ref[...] = (gate / (1.0 + jnp.exp(-gate)) * up).astype(BF)


def hidden_back_kernel(dm0_ref, dm1_ref, w0_ref, w1_ref, gate_up_ref, out_ref):
    half = w1_ref.shape[0]
    d_hidden = product_nt(dm0_ref[...], flat(w0_ref)) + product_nt(dm1_ref[...], w1_ref[...])
    gate = gate_up_ref[:, :half].astype(F32)
    up = gate_up_ref[:, half:].astype(F32)
    sig = 1.0 / (1.0 + jnp.exp(-gate))
    out_ref[:, :half] = (d_hidden * up * sig * (1.0 + gate * (1.0 - sig))).astype(BF)
    out_ref[:, half:] = (d_hidden * gate * sig).astype(BF)


def block_product(left, right, first, count, transposed=False, after=()):
    view = isinstance(right, tuple)
    shape = (right[0].shape[0] * right[1], right[2]) if view else right.shape
    columns = shape[0] if transposed else shape[1]

    def kernel(left_ref, right_ref, out_ref):
        out_ref[...] = (product_nt if transposed else product)(left_ref[...], flat(right_ref)).astype(BF)

    return call(
        kernel, (count,),
        [row_block(left.shape[1], first), resident_view(right) if view else resident(right.shape)], row_block(columns),
        jax.ShapeDtypeStruct((count * BLOCK, columns), BF), 2 * count * BLOCK * left.shape[1] * columns,
        (left, right[0] if view else right), after,
    )


def weight_grad(left, right, after=(), parts=1, spare=0):
    rows, columns = left.shape[1] // parts, right.shape[1]
    size = min(BLOCK, rows)
    steps = rows // size

    def kernel(left_ref, right_ref, out_ref):
        out_ref[0] = product_tn(left_ref[...], right_ref[...]).astype(BF)

    return call(
        kernel, (parts * steps,),
        [pl.BlockSpec((left.shape[0], size), lambda i: (0, i)), resident(right.shape)],
        pl.BlockSpec((1, size, columns), lambda i: (i // steps, i % steps, 0)),
        jax.ShapeDtypeStruct((parts, rows + spare, columns), BF), 2 * left.shape[0] * left.shape[1] * columns,
        (left, right), after,
    )


def ordered(values, after):
    def kernel(in_ref, out_ref):
        out_ref[...] = in_ref[...]

    whole = pl.BlockSpec(values.shape, lambda i: (0,) * values.ndim)
    return call(kernel, (1,), [whole], whole, jax.ShapeDtypeStruct(values.shape, values.dtype), 0, (values,), after)


def beside(left, right, after):
    columns = left.shape[1]

    def kernel(left_ref, right_ref, out_ref):
        out_ref[:, :columns] = left_ref[...]
        out_ref[:, columns:] = right_ref[...]

    whole = [pl.BlockSpec(shape, lambda i: (0, 0)) for shape in (left.shape, right.shape)]
    shape = (left.shape[0], columns + right.shape[1])
    return call(
        kernel, (1,), whole, pl.BlockSpec(shape, lambda i: (0, 0)), jax.ShapeDtypeStruct(shape, left.dtype), 0,
        (left, right), after,
    )


def split_rows(values, which, rows, after=()):
    columns = values.shape[1]
    extra = len(after)

    def kernel(which_ref, mine_ref, given_ref, *refs):
        refs[extra][...] = mine_ref[...]
        refs[extra + 1][...] = given_ref[...]

    width = columns // 2
    return pl.pallas_call(
        kernel,
        grid_spec=pltpu.PrefetchScalarGridSpec(
            num_scalar_prefetch=1,
            grid=(2,),
            in_specs=[
                pl.BlockSpec((rows, width), lambda i, w: (w[0], i)),
                pl.BlockSpec((rows, width), lambda i, w: (1 - w[0], i)),
            ]
            + [pl.BlockSpec(memory_space=pl.ANY)] * extra,
            out_specs=[pl.BlockSpec((rows, width), lambda i, w: (0, i))] * 2,
        ),
        out_shape=[jax.ShapeDtypeStruct((rows, columns), values.dtype)] * 2,
        cost_estimate=cost(0, values, values),
    )(jnp.reshape(which, (1,)).astype(jnp.int32), values, values, *after)


def assemble(pieces, out_shape, rows, columns, steps, spots, place, scalars):
    count = len(pieces)
    outs = len(out_shape)

    def in_map(k, o):
        def index(j, s, scalars):
            at = spots(o, jnp.where(j == k, s, jnp.where(j < k, 0, steps - 1)))
            return at

        return index

    def out_map(o):
        return lambda j, s, scalars: place(o, j, s, scalars)

    def kernel(scalar_ref, *refs):
        j = pl.program_id(0)
        for k in range(count):

            @pl.when(j == k)
            def _():
                for o in range(outs):
                    refs[count * outs + o][...] = refs[k * outs + o][...].astype(F32)

    return pl.pallas_call(
        kernel,
        grid_spec=pltpu.PrefetchScalarGridSpec(
            num_scalar_prefetch=1,
            grid=(count, steps),
            in_specs=[pl.BlockSpec((rows, columns), in_map(k, o)) for k in range(count) for o in range(outs)],
            out_specs=[pl.BlockSpec((rows, columns), out_map(o)) for o in range(outs)],
        ),
        out_shape=out_shape,
        compiler_params=pltpu.CompilerParams(vmem_limit_bytes=VMEM_LIMIT),
        cost_estimate=cost(0, *pieces, *out_shape),
    )(scalars, *[p for p in pieces for _ in range(outs)])


def plane_scatter(make, between=None, lean=False):
    corner_part = make(*PARTS[0], ())
    rows = corner_part.shape[0] // 2
    half = rows // 2
    next_part = make(*PARTS[1], (corner_part,))
    corner = (corner_part[:rows].astype(F32) + swap(corner_part[rows:], "c").astype(F32)).astype(BF)
    if between is not None:
        between((corner, next_part))
    if lean:
        from_a, from_y = None, swap(corner, "y").astype(F32)
    else:
        from_a, from_y = swap(corner[:half], "a").astype(F32), swap(corner[half:], "y").astype(F32)
    a_near = next_part[:rows].astype(F32) + swap(next_part[rows : 2 * rows], "c").astype(F32)
    y_near = next_part[2 * rows : 3 * rows].astype(F32) + swap(next_part[3 * rows :], "c").astype(F32)
    if lean:
        to_a, to_y = (a_near + from_y).astype(BF), y_near.astype(BF)
    else:
        to_a = jnp.concatenate([a_near[:half], a_near[half:] + from_y], axis=0).astype(BF)
        to_y = jnp.concatenate([y_near[:half] + from_a, y_near[half:]], axis=0).astype(BF)
    own_part = make(*PARTS[2], (corner, next_part))
    own = own_part[:rows].astype(F32) + swap(own_part[rows:], "c").astype(F32)
    return own + swap(to_a, "a").astype(F32) + swap(to_y, "y").astype(F32), (to_a, to_y)


def plane_sum_tokens(stats):
    kinds, _, count = stats.shape
    values = stats.reshape(kinds, 2, 2, 2, count)
    for axis, dim in (("a", 1), ("y", 2), ("c", 3)):
        values = values + jnp.flip(swap(values, axis), dim)
    return values.reshape(kinds, 8, count)


def exchange_members(blocks, a, c):
    return exchange_last(*exchange_first(blocks, a), a, c)


def exchange_first(blocks, a):
    both = blocks.reshape((2, 2) + blocks.shape[1:])
    mine = lax.dynamic_index_in_dim(both, a, 0, keepdims=False)
    return mine, swap(lax.dynamic_index_in_dim(both, 1 - a, 0, keepdims=False), "a")


def exchange_last(mine, other, a, c):
    blocks = jax.ShapeDtypeStruct((4,) + mine.shape[1:], mine.dtype)
    both = ordered_pair(mine, other, a)
    mine = lax.dynamic_index_in_dim(both, c, 1, keepdims=False)
    other = swap(lax.dynamic_index_in_dim(both, 1 - c, 1, keepdims=False), "c")
    return ordered_pair(mine, other, c, 1).reshape(blocks.shape)


def spread(pieces):
    both = list(pieces) + [swap(piece, "a") for piece in pieces]
    return both + [swap(piece, "c") for piece in both]


def ordered_pair(mine, other, index, axis=0):
    return jnp.where(index == 0, jnp.stack([mine, other], axis=axis), jnp.stack([other, mine], axis=axis))


def rotation_tables(segments):
    row_index = jnp.arange(MB, dtype=jnp.int32)
    same_seg = segments[:, :, None] == segments[:, None, :]
    allowed = jnp.logical_and(same_seg, row_index[:, None] >= row_index[None, :])
    position = jnp.sum(allowed.astype(jnp.int32), axis=2) - 1
    half_dim = HEAD_DIM // 2
    frequency = THETA ** (-2.0 * jnp.arange(half_dim, dtype=F32) / HEAD_DIM)
    angles = position.astype(F32).reshape(-1, 1) * frequency
    cosine, sine = jnp.cos(angles), jnp.sin(angles)
    return jnp.concatenate([cosine, cosine], axis=1), jnp.concatenate([-sine, sine], axis=1)


def make_body(planes):
    def body(
        block_input, segment_ids, w_query, w_key, w_value, w_out, gain_query, gain_key, gain_attn,
        w_gate, w_up, w_down, gain_mlp, out_cotangent,
    ):
        a = lax.axis_index("a")
        c = lax.axis_index("c")
        z = lax.axis_index("z")
        y = lax.axis_index("y")
        member = a * 2 + c
        pair = member * 2 + y
        own_rows = block_input.shape[0]
        all_rows = own_rows * 8
        shard_rows = w_query.shape[0]
        width = D // 8
        ff_shard = w_down.shape[0]
        quarter = ff_shard // 4
        ff_here = planes * quarter
        blocks = all_rows // BLOCK

        segments = plane_gather_small(segment_ids.reshape(own_rows // MB, MB))
        live = (segment_ids >= 0).astype(F32)[:, None]

        def columns_of(which_y):
            at = (member * 2 + which_y) * width
            return jnp.concatenate(
                [lax.dynamic_slice(w, (0, at), (shard_rows, width)) for w in (w_query, w_key, w_value)], axis=1
            )

        def hidden_columns_of(which_y):
            starts = [((plane * 2 + which_y) * 4 + member) * quarter for plane in range(planes)]
            return jnp.concatenate(
                [lax.dynamic_slice(w, (0, at), (shard_rows, quarter)) for w in (w_gate, w_up) for at in starts], axis=1
            )

        def column_weights(mine, given, more, next_to=()):
            both = ordered_pair(mine, swap(given, "y"), y).reshape(2 * shard_rows, -1)
            return jnp.concatenate([jnp.concatenate([both] + list(next_to), axis=1), more], axis=0)

        def gather_planes(piece):
            return lax.all_gather(piece, "z", axis=0, tiled=False)

        own_gains = jnp.stack([gain_query, gain_key, gain_attn, gain_mlp]).reshape(2, 2 * shard_rows)
        more, next_to = own_gains, []
        if planes == 4:
            out_piece = lax.dynamic_slice(w_out, (member * (shard_rows // 4), 0), (shard_rows // 4, D))
            next_to = [out_piece.reshape(2 * shard_rows, -1)]
        more = jnp.pad(own_gains, ((0, 14), (0, (3 + len(next_to)) * width - 2 * shard_rows)))
        qkv_array = gather_planes(column_weights(columns_of(y), columns_of(1 - y), more, next_to))
        x_near = []
        x_all = plane_gather(block_input, x_near)
        down_pieces = [lax.dynamic_slice(w_down, (member * quarter, n * D // 2), (quarter, D // 2)) for n in range(2)]
        gu_given = ordered(hidden_columns_of(1 - y), x_near)
        gu_array = gather_planes(
            column_weights(
                hidden_columns_of(y), gu_given,
                jnp.concatenate([down_pieces[0][: quarter // 2], down_pieces[0][quarter // 2 :]], axis=1),
            )
        )
        last_down = gather_planes(down_pieces[1]).reshape(ff_here, D // 2)
        qkv_w = (qkv_array, 2 * shard_rows, 3 * width)
        gains = qkv_array[:, 2 * shard_rows : 2 * shard_rows + 2, : 2 * shard_rows].reshape(planes, 4, shard_rows)
        gains = ordered_pair(gains, swap(gains, "y"), y, 1)
        gains = jnp.transpose(gains, (2, 0, 1, 3)).reshape(4, D).astype(F32)
        gain_q = lax.dynamic_slice(gains[0], (pair * width,), (width,))
        gain_k = lax.dynamic_slice(gains[1], (pair * width,), (width,))
        gain_a, gain_m = gains[2], gains[3]
        if planes == 4:
            out_pieces = qkv_array[:, : 2 * shard_rows, 3 * width :].reshape(planes, shard_rows // 4, D)
            out_rows = exchange_members(out_pieces, a, c).reshape(width, D)
        else:
            out_rows = lax.dynamic_slice(
                lax.all_gather(w_out, ("z", "y"), axis=0, tiled=True), (pair * width, 0), (width, D)
            )
        gu_w = (gu_array, 2 * shard_rows, 2 * ff_here)

        shaped = jax.ShapeDtypeStruct
        cosine, sine = rotation_tables(segments)
        qkv, squares = call(
            qkv_kernel, (blocks,), [row_block(D), resident_view(qkv_w)], [row_block(3 * width), stat_block()],
            [shaped((all_rows, 3 * width), F32), shaped((2, all_rows), F32)], 2 * all_rows * D * 3 * width,
            (x_all, qkv_array), (cosine, sine),
        )
        squares = plane_sum_tokens(squares.reshape(2, 8, own_rows)).reshape(2, all_rows)
        seg_row = segments.astype(F32).reshape(1, all_rows)
        gain_qk = jnp.stack([gain_q, gain_k])

        def attention(first, count, after):
            return call(
                attention_kernel, (count,),
                [
                    row_block(3 * width, first), stat_block(first), pl.BlockSpec((1, BLOCK), lambda i: (0, first + i)),
                    row_block(HEAD_DIM, first), row_block(HEAD_DIM, first), resident((2, width)), resident((width, D)),
                ],
                [row_block(3 * width), row_block(width), row_block(D)],
                [shaped((count * BLOCK, cols), BF) for cols in (3 * width, width, D)],
                2 * count * BLOCK * width * (D + 2 * MB),
                (qkv, squares, seg_row, cosine, sine, gain_qk, out_rows), after,
            )

        lows, atts = [], []

        def branch_part(first, count, after):
            low_part, att_part, part = attention(first, count, after)
            lows.append(low_part)
            atts.append(att_part)
            return part

        branch, _ = plane_scatter(branch_part)
        attended = jnp.concatenate(atts, axis=0)
        low = jnp.concatenate(lows, axis=0)

        def row_scale(values):
            return lax.rsqrt(jnp.mean(values * values, axis=-1, keepdims=True) + EPS)

        def norm_back(values, scale_here, gain, upstream):
            n = upstream * gain
            grad = scale_here * n - scale_here**3 * values * jnp.mean(n * values, axis=-1, keepdims=True)
            return grad, jnp.sum(upstream * values * scale_here, axis=0)

        branch_scale = row_scale(branch)
        middle = block_input.astype(F32) + branch * branch_scale * gain_a
        mid_all = plane_gather(middle.astype(BF))

        gate_up, hidden = call(
            gate_up_kernel, (blocks,), [row_block(D), resident_view(gu_w)],
            [row_block(2 * ff_here), row_block(ff_here)],
            [shaped((all_rows, 2 * ff_here), BF), shaped((all_rows, ff_here), BF)], 4 * all_rows * D * ff_here,
            (mid_all, gu_array),
        )
        size, first = quarter // 2, 2 * shard_rows // (quarter // 2)

        def take_kernel(in_ref, out_ref):
            out_ref[...] = in_ref[...]

        first_down = call(
            take_kernel, (2 * planes,), [pl.BlockSpec((1, size, D // 2), lambda i: (i // 2, first, i % 2))],
            pl.BlockSpec((1, size, D // 2), lambda i: (i // 2, i % 2, 0)),
            shaped((planes, quarter, D // 2), BF), 0, (gu_array,), (hidden,),
        )
        down_w = [first_down.reshape(ff_here, D // 2), last_down]
        mixed0, marks = plane_scatter(lambda first, count, after: block_product(hidden, down_w[0], first, count, False, after))
        mixed1, _ = plane_scatter(
            lambda first, count, after: block_product(hidden, down_w[1], first, count, False, after + marks)
        )
        mixed = jnp.concatenate([mixed0, mixed1], axis=1)
        mixed_scale = row_scale(mixed)
        block_output = ((middle + mixed * mixed_scale * gain_m) * live).astype(BF)

        grad_rows = out_cotangent.astype(F32) * live
        d_mixed, d_gain_mlp = norm_back(mixed, mixed_scale, gain_m, grad_rows)
        early = []
        dm_halves = [d_mixed[:, cut].astype(BF) for cut in HALVES]
        dm_all = [plane_gather(dm_halves[0], early)]
        grad_down_parts = [product_tn(hidden, dm_all[0]).astype(BF)]
        dm_all.append(plane_gather(ordered(dm_halves[1], early), hold=grad_down_parts))
        grad_down_parts = grad_down_parts + [product_tn(hidden, dm_all[1]).astype(BF)]

        def plane_sum(values):
            return lax.psum_scatter(values.astype(BF), "z", scatter_dimension=0, tiled=True)

        grad_down = [plane_sum(part) for part in grad_down_parts]
        d_gu = call(
            hidden_back_kernel, (blocks,),
            [row_block(D // 2), row_block(D // 2), resident((ff_here, D // 2)), resident((ff_here, D // 2)),
             row_block(2 * ff_here)],
            row_block(2 * ff_here), shaped((all_rows, 2 * ff_here), BF), 2 * all_rows * D * ff_here,
            (*dm_all, *down_w, gate_up), grad_down_parts,
        )
        down_first = ordered(grad_down[0], (d_gu,))
        grad_gu_part = weight_grad(mid_all, d_gu, (down_first,))[0]
        grad_gu = plane_sum(grad_gu_part)
        d_middle, _ = plane_scatter(
            lambda first, count, after: block_product(d_gu, gu_w, first, count, True, after + (grad_gu_part,))
        )
        scalars = jnp.stack([a, c, y]).astype(jnp.int32)

        def member_of(j_a, j_c, scalars):
            return (scalars[0] ^ j_a) * 2 + (scalars[1] ^ j_c)

        d_middle = grad_rows + d_middle
        down_last = ordered(grad_down[1], (d_middle,))

        d_branch, d_gain_attn = norm_back(branch, branch_scale, gain_a, d_middle)
        def attention_back(first, pieces, filled, after):
            places = []
            for piece in pieces:
                places.append((sum(p.shape[0] for p in pieces[: len(places)]), piece.shape[0]))
            count = sum(rows for _, rows in places) // BLOCK

            def kernel(*refs):
                ins, rest = refs[: len(pieces)], refs[len(pieces) :]
                db_ref = rest[8 + len(filled)]
                for (start, rows), ref in zip(places, ins):

                    @pl.when(pl.program_id(0) == start // BLOCK)
                    def _():
                        db_ref[start % BLOCK : start % BLOCK + rows, :] = ref[...]

                attention_back_kernel(*rest[:8], *rest[8 + len(filled) :])

            return call_back(kernel, first, count, pieces, filled, after)

        def call_back(kernel, first, count, pieces, filled, after):
            known = len(pieces) + 8
            shapes = [
                shaped((all_rows, D), BF), shaped((all_rows, 2 * width), F32), shaped((all_rows, width), BF),
                shaped((2, all_rows), F32), shaped((count, 2, width), F32),
            ]
            anywhere = pl.BlockSpec(memory_space=pl.ANY)
            args = (low, qkv, squares, seg_row, cosine, sine, gain_qk, out_rows)
            extra = len(after)

            def body(*refs):
                kernel(*refs[: known + len(filled)], *refs[known + len(filled) + extra :])

            return pl.pallas_call(
                body,
                grid=(count,),
                in_specs=[resident(piece.shape) for piece in pieces]
                + [
                    row_block(3 * width, first), row_block(2 * width, first), stat_block(first),
                    pl.BlockSpec((1, BLOCK), lambda i: (0, first + i)), row_block(HEAD_DIM, first),
                    row_block(HEAD_DIM, first), resident((2, width)), resident((width, D)),
                ]
                + [anywhere] * (len(filled) + extra),
                out_specs=[
                    row_block(D, first), row_block(2 * width, first), row_block(width, first), stat_block(first),
                    pl.BlockSpec((1, 2, width), lambda i: (i, 0, 0)),
                ],
                out_shape=shapes,
                input_output_aliases={known + k: k for k in range(len(filled))},
                compiler_params=pltpu.CompilerParams(vmem_limit_bytes=58 * 1024 * 1024),
                cost_estimate=cost(2 * count * BLOCK * width * (D + 12 * MB), *pieces),
            )(*pieces, *args, *filled, *after)

        half = own_rows // 2
        db_own = d_branch.astype(BF)
        db_a, db_y = swap(db_own, "a"), swap(db_own, "y")
        *filled, gain_part0 = attention_back(6, [db_own, swap(db_own, "c")], (), (down_last,))
        top = swap(ordered(db_y[:half], (gain_part0,)), "a")
        bottom = swap(ordered(db_a[half:], (gain_part0,)), "y")
        far_a, far_y = swap(db_a, "c"), swap(db_y, "c")
        *filled, gain_part1 = attention_back(2, [db_a, far_a, db_y, far_y], filled, ())
        corner = [top, bottom] + [swap(ordered(piece, (gain_part1,)), "c") for piece in (top, bottom)]
        db_all, n_qk, d_value, dots, gain_part2 = attention_back(0, corner, filled, ())
        gu_mine, gu_given = split_rows(grad_gu, y, shard_rows, (gain_part1, top, bottom))
        grad_down_all = lax.all_gather(beside(down_first, down_last, (gu_mine,)), ("a", "c"), axis=0, tiled=True)
        gain_part = jnp.concatenate([gain_part0, gain_part1, gain_part2], axis=0)
        d_gain_query, d_gain_key = jnp.sum(gain_part, axis=0)
        zero = jnp.zeros((D,), F32)
        totals = jnp.concatenate(
            [
                dots.reshape(2, all_rows // D, D).reshape(-1, D),
                lax.dynamic_update_slice(zero, d_gain_query, (pair * width,))[None],
                lax.dynamic_update_slice(zero, d_gain_key, (pair * width,))[None],
                d_gain_attn[None],
                d_gain_mlp[None],
            ]
        )
        for axis, dim in (("a", 1), ("y", 2), ("c", 3)):
            other = swap(totals, axis)
            turned = jnp.flip(other[:-4].reshape(2, 2, 2, 2, own_rows), dim).reshape(-1, D)
            totals = totals + jnp.concatenate([turned, other[-4:]])
            if axis == "a":
                grad_out = weight_grad(attended, db_all, (totals,))[0]
                if planes == 4:
                    out_mine, out_other = exchange_first(grad_out.reshape(planes, -1, D), a)
        dots, gain_terms = totals[:-4].reshape(2, all_rows), totals[-4:]
        d_qkv = call(
            qkv_back_kernel, (blocks,),
            [row_block(2 * width), row_block(2 * width), stat_block(), stat_block(), row_block(width)],
            row_block(3 * width), shaped((all_rows, 3 * width), BF), 0, (n_qk, qkv, squares, dots, d_value),
            (grad_down_all,),
        )
        gain_rows = jnp.transpose(gain_terms.reshape(4, planes, 2, shard_rows), (1, 2, 0, 3)).reshape(planes, -1)
        more = -(8 * shard_rows) % (3 * width)
        gain_rows = jnp.pad(gain_rows.astype(BF), ((0, 0), (0, more))).reshape(planes, -1, 3 * width)
        gain_rows = jnp.pad(gain_rows, ((0, 0), (0, 16 - gain_rows.shape[1]), (0, 0)))
        grad_qkv_part = weight_grad(x_all, d_qkv, (), planes, 16)
        grad_qkv = plane_sum(
            lax.dynamic_update_slice(grad_qkv_part, gain_rows, (0, 2 * shard_rows, 0)).reshape(-1, 3 * width)
        )
        own_gains = grad_qkv[2 * shard_rows :].reshape(-1)[: 8 * shard_rows].reshape(2, 4, shard_rows)
        own_gains = lax.dynamic_index_in_dim(own_gains, y, 0, keepdims=False).astype(F32)
        if planes == 4:
            grad_out = exchange_last(out_mine, ordered(out_other, (grad_qkv_part,)), a, c).reshape(width, D)
            grad_out = plane_sum(ordered(grad_out, (grad_qkv,)))
        gu_near, gu_other = (swap(ordered(piece, (grad_qkv_part,)), axis) for piece, axis in ((gu_mine, "a"), (gu_given, "y")))
        gu_far = swap(gu_other, "a")
        gu_pieces = [gu_mine, gu_other, gu_near, gu_far]
        gu_pieces += [swap(piece, "c") for piece in gu_pieces]
        def column_pair(j, scalars):
            return member_of((j // 2) % 2, j // 4, scalars), scalars[2] ^ (j % 2)

        if quarter % 128 == 0:
            owners = [column_pair(j, scalars) for j in range(8)]
            places = jnp.stack([jnp.stack([(p * 2 + of_y) * 4 + of for p in range(planes)]) for of, of_y in owners])
            grad_gate, grad_up = assemble_hidden(gu_pieces, 8 * ff_here, places.astype(jnp.int32), quarter, planes)
        else:
            filled = jnp.zeros((shard_rows, 2, planes, 2, 4, quarter), F32)
            for j, piece in enumerate(gu_pieces):
                owner, which_y = column_pair(j, scalars)
                piece = piece.astype(F32).reshape(shard_rows, 2, planes, 1, 1, quarter)
                filled = lax.dynamic_update_slice(filled, piece, (0, 0, 0, which_y, owner, 0))
            grad_gate, grad_up = (filled[:, o].reshape(shard_rows, 8 * ff_here) for o in range(2))

        qkv_mine, qkv_given = split_rows(grad_qkv, y, shard_rows)
        qkv_near, qkv_other = swap(qkv_mine, "a"), swap(qkv_given, "y")
        in_parts = []

        def in_part(first, count, after):
            in_parts.append(block_product(d_qkv, qkv_w, first, count, True, after + (grad_qkv_part,)))
            return in_parts[-1]


        d_input, _ = plane_scatter(in_part, lean=True)
        d_input = d_middle + d_input

        def qkv_place(o, j, s, scalars):
            owner, which_y = column_pair(j, scalars)
            return 0, owner * 2 + which_y

        qkv_far = swap(qkv_other, "a")
        qkv_pieces = [qkv_mine, qkv_other, qkv_near, qkv_far]
        qkv_pieces += [swap(piece, "c") for piece in qkv_pieces]
        grad_query, grad_key, grad_value = assemble(
            qkv_pieces, [shaped((shard_rows, D), F32)] * 3, shard_rows, width, 1,
            lambda o, s: (0, o), qkv_place, scalars,
        )
        if planes == 4:
            (grad_out,) = assemble(
                spread([grad_out]), [shaped((shard_rows, D), F32)], shard_rows // 4, D, 1,
                lambda o, s: (0, 0), lambda o, j, s, scalars: (member_of(j % 2, j // 2, scalars), 0), scalars,
            )
        else:
            whole = lax.dynamic_update_slice(jnp.zeros((D, D), BF), grad_out, (pair * width, 0))
            whole = lax.psum_scatter(whole, ("z", "y"), scatter_dimension=0, tiled=True)
            grad_out = lax.psum(whole, ("a", "c")).astype(F32)

        return (
            block_output,
            d_input,
            grad_query,
            grad_key,
            grad_value,
            grad_out,
            own_gains[0],
            own_gains[1],
            own_gains[2],
            grad_gate,
            grad_up,
            grad_down_all.astype(F32),
            own_gains[3],
        )

    return body


def solution(mesh):
    replicas, shards = mesh.shape["dp"], mesh.shape["fsdp"]
    planes = shards // 2
    fine = Mesh(mesh.devices.reshape(replicas // 2, 2, planes, 2), ("a", "c", "z", "y"))
    tokens = ("a", "c", "z", "y")
    owner = ("z", "y")
    rows, row, wide, vec = P(tokens, None), P(tokens), P(owner, None), P(owner)
    in_specs = (rows, row, wide, wide, wide, wide, vec, vec, vec, wide, wide, wide, vec, rows)
    out_specs = (rows, rows, wide, wide, wide, wide, vec, vec, vec, wide, wide, wide, vec)
    return jax.shard_map(make_body(planes), mesh=fine, in_specs=in_specs, out_specs=out_specs, check_vma=False)
```

```python
import jax
import jax.numpy as jnp
from jax import lax
from jax.experimental import pallas as pl
from jax.experimental.pallas import tpu as pltpu
from jax.sharding import Mesh, PartitionSpec as P

D = 2048
HEADS = 16
HEAD_DIM = 128
MB = 128
EPS = 1e-06
THETA = 500000.0
NEG = -1e30
BF = jnp.bfloat16
F32 = jnp.float32
SWAP = [(0, 1), (1, 0)]
BLOCK = 256
PARTS = ((0, 2), (2, 4), (6, 2))
VMEM_LIMIT = 40 * 1024 * 1024


def cost(flops, *arrays):
    moved = sum(v.size * v.dtype.itemsize for v in arrays)
    return pl.CostEstimate(flops=flops, bytes_accessed=moved, transcendentals=0)
HALVES = (slice(0, D // 2), slice(D // 2, D))


def product(left_rows, right_rows):
    return jnp.dot(left_rows, right_rows, preferred_element_type=F32)


def product_nt(left_rows, right_rows):
    return lax.dot_general(left_rows, right_rows, (((1,), (1,)), ((), ())), preferred_element_type=F32)


def product_tn(left_rows, right_rows):
    return lax.dot_general(left_rows, right_rows, (((0,), (0,)), ((), ())), preferred_element_type=F32)


def swap(values, axis):
    return lax.ppermute(values, axis, SWAP)


def plane_gather(rows, early=None, hold=()):
    half = rows.shape[0] // 2
    by_a = swap(rows, "a")
    by_y = swap(rows, "y")
    if early is not None:
        early.extend((by_a, by_y))
    top, bottom = by_y[:half], by_a[half:]
    if hold:
        top, bottom = ordered(top, hold), ordered(bottom, hold)
    top = swap(top, "a")
    bottom = swap(bottom, "y")
    far_a, far_y, far_top, far_bottom = (swap(piece, "c") for piece in (by_a, by_y, top, bottom))
    pieces = [top, bottom, far_top, far_bottom, by_a, far_a, by_y, far_y, rows, swap(rows, "c")]
    return jnp.concatenate(pieces, axis=0)


def plane_gather_small(values):
    values = jnp.concatenate([values, swap(values, "c")], axis=0)
    for axis in ("y", "a"):
        values = jnp.concatenate([swap(values, axis), values], axis=0)
    return values


def assemble_hidden(pieces, columns, places, quarter, planes):
    rows, width = pieces[0].shape
    count = len(pieces)
    parts = 2 * planes

    def kernel(places_ref, *refs):
        ins, outs, held, sems = refs[:count], refs[count : count + 2], refs[count + 2], refs[count + 3]

        def copies(k):
            for n in range(parts):
                at = pl.multiple_of(places_ref[k, n % planes] * quarter, quarter)
                yield pltpu.make_async_copy(
                    held.at[k % 2, :, n * quarter : (n + 1) * quarter],
                    outs[n // planes].at[:, pl.ds(at, quarter)],
                    sems.at[k % 2, n],
                )

        for k in range(count):
            if k >= 2:
                for copy in copies(k - 2):
                    copy.wait()
            held[k % 2] = ins[k][...].astype(F32)
            for copy in copies(k):
                copy.start()
        for k in range(count - 2, count):
            for copy in copies(k):
                copy.wait()

    return pl.pallas_call(
        kernel,
        grid_spec=pltpu.PrefetchScalarGridSpec(
            num_scalar_prefetch=1,
            grid=(1,),
            in_specs=[pl.BlockSpec((rows, width), lambda i, s: (0, 0), pipeline_mode=pl.Buffered(1))] * count,
            out_specs=[pl.BlockSpec(memory_space=pl.ANY)] * 2,
            scratch_shapes=[pltpu.VMEM((2, rows, width), F32), pltpu.SemaphoreType.DMA((2, parts))],
        ),
        out_shape=[jax.ShapeDtypeStruct((rows, columns), F32)] * 2,
        compiler_params=pltpu.CompilerParams(vmem_limit_bytes=VMEM_LIMIT),
        cost_estimate=cost(0, *pieces, *pieces, *pieces),
    )(places, *pieces)


def resident(shape):
    return pl.BlockSpec(shape, lambda i: (0,) * len(shape), pipeline_mode=pl.Buffered(1))


def resident_view(view):
    array, rows, columns = view
    return resident((array.shape[0], rows, columns))


def flat(ref):
    value = ref[...]
    return value.reshape(-1, value.shape[-1]) if value.ndim == 3 else value


def row_block(columns, first=0):
    return pl.BlockSpec((BLOCK, columns), lambda i: (first + i, 0))


def stat_block(first=0):
    return pl.BlockSpec((2, BLOCK), lambda i: (0, first + i))


def call(kernel, grid, in_specs, out_specs, out_shape, flops, args, after=(), through=()):
    outs = isinstance(out_shape, (list, tuple))
    out_shape = list(out_shape) if outs else [out_shape]
    out_specs = list(out_specs) if outs else [out_specs]
    extra = len(after) + len(through)
    known = len(args)
    results = len(out_shape)

    def body(*refs):
        kernel(*refs[:known], *refs[known + extra : known + extra + results])

    anywhere = pl.BlockSpec(memory_space=pl.ANY)
    given = pl.pallas_call(
        body,
        grid=grid,
        in_specs=list(in_specs) + [anywhere] * extra,
        out_specs=out_specs + [anywhere] * len(through),
        out_shape=out_shape + [jax.ShapeDtypeStruct(v.shape, v.dtype) for v in through],
        input_output_aliases={known + len(after) + k: results + k for k in range(len(through))},
        compiler_params=pltpu.CompilerParams(vmem_limit_bytes=VMEM_LIMIT),
        cost_estimate=cost(flops, *args, *out_shape),
    )(*args, *after, *through)
    own = given[:results] if outs else given[0]
    return (own, *given[results:]) if through else own


def eye():
    shape = (MB, MB)
    return lax.broadcasted_iota(jnp.int32, shape, 0) == lax.broadcasted_iota(jnp.int32, shape, 1)


def as_column(row):
    return jnp.sum(jnp.where(eye(), row, 0.0), axis=1, keepdims=True)


def as_row(column):
    return jnp.sum(jnp.where(eye(), column, 0.0), axis=0, keepdims=True)


def allowed_pairs(segment_row):
    shape = (MB, MB)
    earlier = lax.broadcasted_iota(jnp.int32, shape, 0) >= lax.broadcasted_iota(jnp.int32, shape, 1)
    return jnp.logical_and(as_column(segment_row) == segment_row, earlier)


def qkv_kernel(x_ref, w_ref, qkv_ref, squares_ref):
    width = w_ref.shape[2] // 3
    qkv = product(x_ref[...], flat(w_ref))
    qkv_ref[...] = qkv
    for kind in range(2):
        part = qkv[:, kind * width : (kind + 1) * width]
        total = jnp.sum(part * part, axis=1, keepdims=True)
        for m in range(BLOCK // MB):
            squares_ref[kind : kind + 1, m * MB : (m + 1) * MB] = as_row(total[m * MB : (m + 1) * MB])


def head_slots(width):
    for m in range(BLOCK // MB):
        for h in range(width // HEAD_DIM):
            starts = [kind * width + h * HEAD_DIM for kind in range(3)]
            yield m, h, slice(m * MB, (m + 1) * MB), [slice(at, at + HEAD_DIM) for at in starts]


def masked_softmax(queries, keys, allowed):
    scores = [product_nt(query, key) * HEAD_DIM**-0.5 for query, key in zip(queries, keys)]
    scores = [jnp.where(mask, score, NEG) for mask, score in zip(allowed, scores)]
    tops = [jnp.max(score, axis=1, keepdims=True) for score in scores]
    powers = [jnp.exp(score - top) for score, top in zip(scores, tops)]
    sums = [jnp.sum(power, axis=1, keepdims=True) for power in powers]
    return [power / total for power, total in zip(powers, sums)]


def attention_kernel(qkv_ref, squares_ref, seg_ref, cos_ref, sin_ref, gain_ref, out_ref, low_ref, att_ref, part_ref):
    width = gain_ref.shape[1]
    scales = lax.rsqrt(squares_ref[...] / D + EPS)
    slots = list(head_slots(width))
    masks, columns = [], []
    for m in range(BLOCK // MB):
        rows = slice(m * MB, (m + 1) * MB)
        masks.append(allowed_pairs(seg_ref[:, rows]))
        columns.append([as_column(scales[kind : kind + 1, rows]) for kind in range(2)])
    lows = [[], [], []]
    for kind in range(2):
        for m, h, rows, ats in slots:
            gain = gain_ref[kind : kind + 1, h * HEAD_DIM : (h + 1) * HEAD_DIM]
            u = qkv_ref[rows, ats[kind]] * columns[m][kind] * gain
            lows[kind].append((u * cos_ref[rows, :] + pltpu.roll(u, HEAD_DIM // 2, 1) * sin_ref[rows, :]).astype(BF))
    lows[2] = [qkv_ref[rows, ats[2]].astype(BF) for m, h, rows, ats in slots]
    probs = masked_softmax(lows[0], lows[1], [masks[m] for m, *_ in slots])
    outs = [product(prob.astype(BF), value).astype(BF) for prob, value in zip(probs, lows[2])]
    for n, (m, h, rows, ats) in enumerate(slots):
        for kind in range(3):
            low_ref[rows, ats[kind]] = lows[kind][n]
        att_ref[rows, h * HEAD_DIM : (h + 1) * HEAD_DIM] = outs[n]
    part_ref[...] = product(att_ref[...], out_ref[...]).astype(BF)


def attention_back_kernel(
    low_ref, qkv_ref, squares_ref, seg_ref, cos_ref, sin_ref, gain_ref, out_ref, db_ref,
    n_ref, dv_ref, dots_ref, gain_part_ref,
):
    width = gain_ref.shape[1]
    scales = lax.rsqrt(squares_ref[...] / D + EPS)
    slots = list(head_slots(width))
    masks, columns = [], []
    for m in range(BLOCK // MB):
        rows = slice(m * MB, (m + 1) * MB)
        masks.append(allowed_pairs(seg_ref[:, rows]))
        columns.append([as_column(scales[kind : kind + 1, rows]) for kind in range(2)])
    queries, keys, values = ([low_ref[rows, ats[kind]] for m, h, rows, ats in slots] for kind in range(3))
    d_att = product_nt(db_ref[...], out_ref[...]).astype(BF)
    d_outs = [d_att[rows, h * HEAD_DIM : (h + 1) * HEAD_DIM] for m, h, rows, ats in slots]
    d_probs = [product_nt(d_out, value) for d_out, value in zip(d_outs, values)]
    probs = masked_softmax(queries, keys, [masks[m] for m, *_ in slots])
    d_values = [product_tn(prob.astype(BF), d_out).astype(BF) for prob, d_out in zip(probs, d_outs)]
    inner = [jnp.sum(prob * d_prob, axis=1, keepdims=True) for prob, d_prob in zip(probs, d_probs)]
    d_scores = [(prob * (d_prob - dot)).astype(BF) for prob, d_prob, dot in zip(probs, d_probs, inner)]
    grads = [
        [product(score, key) for score, key in zip(d_scores, keys)],
        [product_tn(score, query) for score, query in zip(d_scores, queries)],
    ]
    dots = [[jnp.zeros((MB, 1), F32) for _ in range(2)] for _ in range(BLOCK // MB)]
    terms = [[jnp.zeros((1, HEAD_DIM), F32) for _ in range(width // HEAD_DIM)] for _ in range(2)]
    for kind in range(2):
        for n, (m, h, rows, ats) in enumerate(slots):
            u = grads[kind][n] * HEAD_DIM**-0.5
            u = u * cos_ref[rows, :] - pltpu.roll(u, HEAD_DIM // 2, 1) * sin_ref[rows, :]
            raw = qkv_ref[rows, ats[kind]]
            grad = u * gain_ref[kind : kind + 1, h * HEAD_DIM : (h + 1) * HEAD_DIM]
            n_ref[rows, ats[kind]] = grad
            dots[m][kind] += jnp.sum(grad * raw, axis=1, keepdims=True)
            terms[kind][h] += jnp.sum(u * (raw * columns[m][kind]), axis=0, keepdims=True)
    for n, (m, h, rows, ats) in enumerate(slots):
        dv_ref[rows, h * HEAD_DIM : (h + 1) * HEAD_DIM] = d_values[n]
    for kind in range(2):
        for m in range(BLOCK // MB):
            dots_ref[kind : kind + 1, m * MB : (m + 1) * MB] = as_row(dots[m][kind])
        for h in range(width // HEAD_DIM):
            gain_part_ref[0, kind : kind + 1, h * HEAD_DIM : (h + 1) * HEAD_DIM] = terms[kind][h]


def qkv_back_kernel(n_ref, qkv_ref, squares_ref, dots_ref, dv_ref, out_ref):
    width = dv_ref.shape[1]
    scales = lax.rsqrt(squares_ref[...] / D + EPS)
    factors = scales * scales * scales * dots_ref[...] / D
    for m in range(BLOCK // MB):
        rows = slice(m * MB, (m + 1) * MB)
        for kind in range(2):
            at = slice(kind * width, (kind + 1) * width)
            near = as_column(scales[kind : kind + 1, rows])
            far = as_column(factors[kind : kind + 1, rows])
            out_ref[rows, at] = (near * n_ref[rows, at] - far * qkv_ref[rows, at]).astype(BF)
    out_ref[:, 2 * width :] = dv_ref[...]


def gate_up_kernel(mid_ref, w_ref, *refs):
    gate_up_ref, hidden_ref = refs[1:3] if len(refs) > 2 else refs
    if len(refs) > 2:
        refs[3][...] = refs[0][...]
    half = hidden_ref.shape[1]
    both = product(mid_ref[...], flat(w_ref))
    gate, up = both[:, :half], both[:, half:]
    gate_up_ref[...] = both.astype(BF)
    hidden_ref[...] = (gate / (1.0 + jnp.exp(-gate)) * up).astype(BF)


def hidden_back_kernel(dm0_ref, dm1_ref, w0_ref, w1_ref, gate_up_ref, out_ref):
    half = w1_ref.shape[0]
    d_hidden = product_nt(dm0_ref[...], flat(w0_ref)) + product_nt(dm1_ref[...], w1_ref[...])
    gate = gate_up_ref[:, :half].astype(F32)
    up = gate_up_ref[:, half:].astype(F32)
    sig = 1.0 / (1.0 + jnp.exp(-gate))
    out_ref[:, :half] = (d_hidden * up * sig * (1.0 + gate * (1.0 - sig))).astype(BF)
    out_ref[:, half:] = (d_hidden * gate * sig).astype(BF)


def block_product(left, right, first, count, transposed=False, after=()):
    view = isinstance(right, tuple)
    shape = (right[0].shape[0] * right[1], right[2]) if view else right.shape
    columns = shape[0] if transposed else shape[1]

    def kernel(left_ref, right_ref, out_ref):
        out_ref[...] = (product_nt if transposed else product)(left_ref[...], flat(right_ref)).astype(BF)

    return call(
        kernel, (count,),
        [row_block(left.shape[1], first), resident_view(right) if view else resident(right.shape)], row_block(columns),
        jax.ShapeDtypeStruct((count * BLOCK, columns), BF), 2 * count * BLOCK * left.shape[1] * columns,
        (left, right[0] if view else right), after,
    )


def weight_grad(left, right, after=(), parts=1, spare=0):
    rows, columns = left.shape[1] // parts, right.shape[1]
    size = min(BLOCK, rows)
    steps = rows // size

    def kernel(left_ref, right_ref, out_ref):
        out_ref[0] = product_tn(left_ref[...], right_ref[...]).astype(BF)

    return call(
        kernel, (parts * steps,),
        [pl.BlockSpec((left.shape[0], size), lambda i: (0, i)), resident(right.shape)],
        pl.BlockSpec((1, size, columns), lambda i: (i // steps, i % steps, 0)),
        jax.ShapeDtypeStruct((parts, rows + spare, columns), BF), 2 * left.shape[0] * left.shape[1] * columns,
        (left, right), after,
    )


def ordered(values, after):
    def kernel(in_ref, out_ref):
        out_ref[...] = in_ref[...]

    whole = pl.BlockSpec(values.shape, lambda i: (0,) * values.ndim)
    return call(kernel, (1,), [whole], whole, jax.ShapeDtypeStruct(values.shape, values.dtype), 0, (values,), after)


def beside(left, right, after):
    columns = left.shape[1]

    def kernel(left_ref, right_ref, out_ref):
        out_ref[:, :columns] = left_ref[...]
        out_ref[:, columns:] = right_ref[...]

    whole = [pl.BlockSpec(shape, lambda i: (0, 0)) for shape in (left.shape, right.shape)]
    shape = (left.shape[0], columns + right.shape[1])
    return call(
        kernel, (1,), whole, pl.BlockSpec(shape, lambda i: (0, 0)), jax.ShapeDtypeStruct(shape, left.dtype), 0,
        (left, right), after,
    )


def split_rows(values, which, rows, after=()):
    columns = values.shape[1]
    extra = len(after)

    def kernel(which_ref, mine_ref, given_ref, *refs):
        refs[extra][...] = mine_ref[...]
        refs[extra + 1][...] = given_ref[...]

    width = columns // 2
    return pl.pallas_call(
        kernel,
        grid_spec=pltpu.PrefetchScalarGridSpec(
            num_scalar_prefetch=1,
            grid=(2,),
            in_specs=[
                pl.BlockSpec((rows, width), lambda i, w: (w[0], i)),
                pl.BlockSpec((rows, width), lambda i, w: (1 - w[0], i)),
            ]
            + [pl.BlockSpec(memory_space=pl.ANY)] * extra,
            out_specs=[pl.BlockSpec((rows, width), lambda i, w: (0, i))] * 2,
        ),
        out_shape=[jax.ShapeDtypeStruct((rows, columns), values.dtype)] * 2,
        cost_estimate=cost(0, values, values),
    )(jnp.reshape(which, (1,)).astype(jnp.int32), values, values, *after)


def assemble(pieces, out_shape, rows, columns, steps, spots, place, scalars):
    count = len(pieces)
    outs = len(out_shape)

    def in_map(k, o):
        def index(j, s, scalars):
            at = spots(o, jnp.where(j == k, s, jnp.where(j < k, 0, steps - 1)))
            return at

        return index

    def out_map(o):
        return lambda j, s, scalars: place(o, j, s, scalars)

    def kernel(scalar_ref, *refs):
        j = pl.program_id(0)
        for k in range(count):

            @pl.when(j == k)
            def _():
                for o in range(outs):
                    refs[count * outs + o][...] = refs[k * outs + o][...].astype(F32)

    return pl.pallas_call(
        kernel,
        grid_spec=pltpu.PrefetchScalarGridSpec(
            num_scalar_prefetch=1,
            grid=(count, steps),
            in_specs=[pl.BlockSpec((rows, columns), in_map(k, o)) for k in range(count) for o in range(outs)],
            out_specs=[pl.BlockSpec((rows, columns), out_map(o)) for o in range(outs)],
        ),
        out_shape=out_shape,
        compiler_params=pltpu.CompilerParams(vmem_limit_bytes=VMEM_LIMIT),
        cost_estimate=cost(0, *pieces, *out_shape),
    )(scalars, *[p for p in pieces for _ in range(outs)])


def plane_scatter(make, between=None, lean=False):
    corner_part = make(*PARTS[0], ())
    rows = corner_part.shape[0] // 2
    half = rows // 2
    next_part = make(*PARTS[1], (corner_part,))
    corner = (corner_part[:rows].astype(F32) + swap(corner_part[rows:], "c").astype(F32)).astype(BF)
    if between is not None:
        between((corner, next_part))
    if lean:
        from_a, from_y = None, swap(corner, "y").astype(F32)
    else:
        from_a, from_y = swap(corner[:half], "a").astype(F32), swap(corner[half:], "y").astype(F32)
    a_near = next_part[:rows].astype(F32) + swap(next_part[rows : 2 * rows], "c").astype(F32)
    y_near = next_part[2 * rows : 3 * rows].astype(F32) + swap(next_part[3 * rows :], "c").astype(F32)
    if lean:
        to_a, to_y = (a_near + from_y).astype(BF), y_near.astype(BF)
    else:
        to_a = jnp.concatenate([a_near[:half], a_near[half:] + from_y], axis=0).astype(BF)
        to_y = jnp.concatenate([y_near[:half] + from_a, y_near[half:]], axis=0).astype(BF)
    own_part = make(*PARTS[2], (corner, next_part))
    own = own_part[:rows].astype(F32) + swap(own_part[rows:], "c").astype(F32)
    return own + swap(to_a, "a").astype(F32) + swap(to_y, "y").astype(F32), (to_a, to_y)


def plane_sum_tokens(stats):
    kinds, _, count = stats.shape
    values = stats.reshape(kinds, 2, 2, 2, count)
    for axis, dim in (("a", 1), ("y", 2), ("c", 3)):
        values = values + jnp.flip(swap(values, axis), dim)
    return values.reshape(kinds, 8, count)


def exchange_members(blocks, a, c):
    return exchange_last(*exchange_first(blocks, a), a, c)


def exchange_first(blocks, a):
    both = blocks.reshape((2, 2) + blocks.shape[1:])
    mine = lax.dynamic_index_in_dim(both, a, 0, keepdims=False)
    return mine, swap(lax.dynamic_index_in_dim(both, 1 - a, 0, keepdims=False), "a")


def exchange_last(mine, other, a, c):
    blocks = jax.ShapeDtypeStruct((4,) + mine.shape[1:], mine.dtype)
    both = ordered_pair(mine, other, a)
    mine = lax.dynamic_index_in_dim(both, c, 1, keepdims=False)
    other = swap(lax.dynamic_index_in_dim(both, 1 - c, 1, keepdims=False), "c")
    return ordered_pair(mine, other, c, 1).reshape(blocks.shape)


def spread(pieces):
    both = list(pieces) + [swap(piece, "a") for piece in pieces]
    return both + [swap(piece, "c") for piece in both]


def ordered_pair(mine, other, index, axis=0):
    return jnp.where(index == 0, jnp.stack([mine, other], axis=axis), jnp.stack([other, mine], axis=axis))


def rotation_tables(segments):
    row_index = jnp.arange(MB, dtype=jnp.int32)
    same_seg = segments[:, :, None] == segments[:, None, :]
    allowed = jnp.logical_and(same_seg, row_index[:, None] >= row_index[None, :])
    position = jnp.sum(allowed.astype(jnp.int32), axis=2) - 1
    half_dim = HEAD_DIM // 2
    frequency = THETA ** (-2.0 * jnp.arange(half_dim, dtype=F32) / HEAD_DIM)
    angles = position.astype(F32).reshape(-1, 1) * frequency
    cosine, sine = jnp.cos(angles), jnp.sin(angles)
    return jnp.concatenate([cosine, cosine], axis=1), jnp.concatenate([-sine, sine], axis=1)


def make_body(planes):
    def body(
        block_input, segment_ids, w_query, w_key, w_value, w_out, gain_query, gain_key, gain_attn,
        w_gate, w_up, w_down, gain_mlp, out_cotangent,
    ):
        a = lax.axis_index("a")
        c = lax.axis_index("c")
        z = lax.axis_index("z")
        y = lax.axis_index("y")
        member = a * 2 + c
        pair = member * 2 + y
        own_rows = block_input.shape[0]
        all_rows = own_rows * 8
        shard_rows = w_query.shape[0]
        width = D // 8
        ff_shard = w_down.shape[0]
        quarter = ff_shard // 4
        ff_here = planes * quarter
        blocks = all_rows // BLOCK

        segments = plane_gather_small(segment_ids.reshape(own_rows // MB, MB))
        live = (segment_ids >= 0).astype(F32)[:, None]

        def columns_of(which_y):
            at = (member * 2 + which_y) * width
            return jnp.concatenate(
                [lax.dynamic_slice(w, (0, at), (shard_rows, width)) for w in (w_query, w_key, w_value)], axis=1
            )

        def hidden_columns_of(which_y):
            starts = [((plane * 2 + which_y) * 4 + member) * quarter for plane in range(planes)]
            return jnp.concatenate(
                [lax.dynamic_slice(w, (0, at), (shard_rows, quarter)) for w in (w_gate, w_up) for at in starts], axis=1
            )

        def column_weights(mine, given, more, next_to=()):
            both = ordered_pair(mine, swap(given, "y"), y).reshape(2 * shard_rows, -1)
            return jnp.concatenate([jnp.concatenate([both] + list(next_to), axis=1), more], axis=0)

        def gather_planes(piece):
            return lax.all_gather(piece, "z", axis=0, tiled=False)

        own_gains = jnp.stack([gain_query, gain_key, gain_attn, gain_mlp]).reshape(2, 2 * shard_rows)
        more, next_to = own_gains, []
        if planes == 4:
            out_piece = lax.dynamic_slice(w_out, (member * (shard_rows // 4), 0), (shard_rows // 4, D))
            next_to = [out_piece.reshape(2 * shard_rows, -1)]
        more = jnp.pad(own_gains, ((0, 14), (0, (3 + len(next_to)) * width - 2 * shard_rows)))
        qkv_array = gather_planes(column_weights(columns_of(y), columns_of(1 - y), more, next_to))
        x_near = []
        x_all = plane_gather(block_input, x_near)
        down_pieces = [lax.dynamic_slice(w_down, (member * quarter, n * D // 2), (quarter, D // 2)) for n in range(2)]
        gu_given = ordered(hidden_columns_of(1 - y), x_near)
        gu_array = gather_planes(
            column_weights(
                hidden_columns_of(y), gu_given,
                jnp.concatenate([down_pieces[0][: quarter // 2], down_pieces[0][quarter // 2 :]], axis=1),
            )
        )
        last_down = gather_planes(down_pieces[1]).reshape(ff_here, D // 2)
        qkv_w = (qkv_array, 2 * shard_rows, 3 * width)
        gains = qkv_array[:, 2 * shard_rows : 2 * shard_rows + 2, : 2 * shard_rows].reshape(planes, 4, shard_rows)
        gains = ordered_pair(gains, swap(gains, "y"), y, 1)
        gains = jnp.transpose(gains, (2, 0, 1, 3)).reshape(4, D).astype(F32)
        gain_q = lax.dynamic_slice(gains[0], (pair * width,), (width,))
        gain_k = lax.dynamic_slice(gains[1], (pair * width,), (width,))
        gain_a, gain_m = gains[2], gains[3]
        if planes == 4:
            out_pieces = qkv_array[:, : 2 * shard_rows, 3 * width :].reshape(planes, shard_rows // 4, D)
            out_rows = exchange_members(out_pieces, a, c).reshape(width, D)
        else:
            out_rows = lax.dynamic_slice(
                lax.all_gather(w_out, ("z", "y"), axis=0, tiled=True), (pair * width, 0), (width, D)
            )
        gu_w = (gu_array, 2 * shard_rows, 2 * ff_here)

        shaped = jax.ShapeDtypeStruct
        cosine, sine = rotation_tables(segments)
        qkv, squares = call(
            qkv_kernel, (blocks,), [row_block(D), resident_view(qkv_w)], [row_block(3 * width), stat_block()],
            [shaped((all_rows, 3 * width), F32), shaped((2, all_rows), F32)], 2 * all_rows * D * 3 * width,
            (x_all, qkv_array), (cosine, sine),
        )
        squares = plane_sum_tokens(squares.reshape(2, 8, own_rows)).reshape(2, all_rows)
        seg_row = segments.astype(F32).reshape(1, all_rows)
        gain_qk = jnp.stack([gain_q, gain_k])

        def attention(first, count, after):
            return call(
                attention_kernel, (count,),
                [
                    row_block(3 * width, first), stat_block(first), pl.BlockSpec((1, BLOCK), lambda i: (0, first + i)),
                    row_block(HEAD_DIM, first), row_block(HEAD_DIM, first), resident((2, width)), resident((width, D)),
                ],
                [row_block(3 * width), row_block(width), row_block(D)],
                [shaped((count * BLOCK, cols), BF) for cols in (3 * width, width, D)],
                2 * count * BLOCK * width * (D + 2 * MB),
                (qkv, squares, seg_row, cosine, sine, gain_qk, out_rows), after,
            )

        lows, atts = [], []

        def branch_part(first, count, after):
            low_part, att_part, part = attention(first, count, after)
            lows.append(low_part)
            atts.append(att_part)
            return part

        branch, _ = plane_scatter(branch_part)
        attended = jnp.concatenate(atts, axis=0)
        low = jnp.concatenate(lows, axis=0)

        def row_scale(values):
            return lax.rsqrt(jnp.mean(values * values, axis=-1, keepdims=True) + EPS)

        def norm_back(values, scale_here, gain, upstream):
            n = upstream * gain
            grad = scale_here * n - scale_here**3 * values * jnp.mean(n * values, axis=-1, keepdims=True)
            return grad, jnp.sum(upstream * values * scale_here, axis=0)

        branch_scale = row_scale(branch)
        middle = block_input.astype(F32) + branch * branch_scale * gain_a
        mid_all = plane_gather(middle.astype(BF))

        size, first = quarter // 2, 2 * shard_rows // (quarter // 2)
        half_in = pl.BlockSpec((1, size, D // 2), lambda i: (i // 2, first, i % 2))
        half_out = pl.BlockSpec((1, size, D // 2), lambda i: (i // 2, i % 2, 0))
        half_shape = shaped((planes, quarter, D // 2), BF)
        together = blocks == 2 * planes
        gate_up, hidden, *first_down = call(
            gate_up_kernel, (blocks,), [row_block(D), resident_view(gu_w)] + [half_in] * together,
            [row_block(2 * ff_here), row_block(ff_here)] + [half_out] * together,
            [shaped((all_rows, 2 * ff_here), BF), shaped((all_rows, ff_here), BF)] + [half_shape] * together,
            4 * all_rows * D * ff_here, (mid_all, gu_array) + (gu_array,) * together,
        )
        if not together:

            def take_kernel(in_ref, out_ref):
                out_ref[...] = in_ref[...]

            first_down = call(take_kernel, (2 * planes,), [half_in], [half_out], [half_shape], 0, (gu_array,), (hidden,))
        down_w = [first_down[0].reshape(ff_here, D // 2), last_down]
        mixed0, marks = plane_scatter(lambda first, count, after: block_product(hidden, down_w[0], first, count, False, after))
        mixed1, _ = plane_scatter(
            lambda first, count, after: block_product(hidden, down_w[1], first, count, False, after + marks)
        )
        mixed = jnp.concatenate([mixed0, mixed1], axis=1)
        mixed_scale = row_scale(mixed)
        block_output = ((middle + mixed * mixed_scale * gain_m) * live).astype(BF)

        grad_rows = out_cotangent.astype(F32) * live
        d_mixed, d_gain_mlp = norm_back(mixed, mixed_scale, gain_m, grad_rows)
        early = []
        dm_halves = [d_mixed[:, cut].astype(BF) for cut in HALVES]
        dm_all = [plane_gather(dm_halves[0], early)]
        grad_down_parts = [product_tn(hidden, dm_all[0]).astype(BF)]
        dm_all.append(plane_gather(ordered(dm_halves[1], early), hold=grad_down_parts))
        grad_down_parts = grad_down_parts + [product_tn(hidden, dm_all[1]).astype(BF)]

        def plane_sum(values):
            return lax.psum_scatter(values.astype(BF), "z", scatter_dimension=0, tiled=True)

        grad_down = [plane_sum(part) for part in grad_down_parts]
        d_gu = call(
            hidden_back_kernel, (blocks,),
            [row_block(D // 2), row_block(D // 2), resident((ff_here, D // 2)), resident((ff_here, D // 2)),
             row_block(2 * ff_here)],
            row_block(2 * ff_here), shaped((all_rows, 2 * ff_here), BF), 2 * all_rows * D * ff_here,
            (*dm_all, *down_w, gate_up), grad_down_parts[:1],
        )
        down_first = ordered(grad_down[0], (d_gu,))
        grad_gu_part = weight_grad(mid_all, d_gu, (down_first,))[0]
        grad_gu = plane_sum(grad_gu_part)
        d_middle, _ = plane_scatter(
            lambda first, count, after: block_product(d_gu, gu_w, first, count, True, after + (grad_gu_part,))
        )
        scalars = jnp.stack([a, c, y]).astype(jnp.int32)

        def member_of(j_a, j_c, scalars):
            return (scalars[0] ^ j_a) * 2 + (scalars[1] ^ j_c)

        d_middle = grad_rows + d_middle
        down_last = ordered(grad_down[1], (d_middle,))

        d_branch, d_gain_attn = norm_back(branch, branch_scale, gain_a, d_middle)
        def attention_back(first, pieces, filled, after):
            places = []
            for piece in pieces:
                places.append((sum(p.shape[0] for p in pieces[: len(places)]), piece.shape[0]))
            count = sum(rows for _, rows in places) // BLOCK

            def kernel(*refs):
                ins, rest = refs[: len(pieces)], refs[len(pieces) :]
                db_ref = rest[8 + len(filled)]
                for (start, rows), ref in zip(places, ins):

                    @pl.when(pl.program_id(0) == start // BLOCK)
                    def _():
                        db_ref[start % BLOCK : start % BLOCK + rows, :] = ref[...]

                attention_back_kernel(*rest[:8], *rest[8 + len(filled) :])

            return call_back(kernel, first, count, pieces, filled, after)

        def call_back(kernel, first, count, pieces, filled, after):
            known = len(pieces) + 8
            shapes = [
                shaped((all_rows, D), BF), shaped((all_rows, 2 * width), F32), shaped((all_rows, width), BF),
                shaped((2, all_rows), F32), shaped((count, 2, width), F32),
            ]
            anywhere = pl.BlockSpec(memory_space=pl.ANY)
            args = (low, qkv, squares, seg_row, cosine, sine, gain_qk, out_rows)
            extra = len(after)

            def body(*refs):
                kernel(*refs[: known + len(filled)], *refs[known + len(filled) + extra :])

            return pl.pallas_call(
                body,
                grid=(count,),
                in_specs=[resident(piece.shape) for piece in pieces]
                + [
                    row_block(3 * width, first), row_block(2 * width, first), stat_block(first),
                    pl.BlockSpec((1, BLOCK), lambda i: (0, first + i)), row_block(HEAD_DIM, first),
                    row_block(HEAD_DIM, first), resident((2, width)), resident((width, D)),
                ]
                + [anywhere] * (len(filled) + extra),
                out_specs=[
                    row_block(D, first), row_block(2 * width, first), row_block(width, first), stat_block(first),
                    pl.BlockSpec((1, 2, width), lambda i: (i, 0, 0)),
                ],
                out_shape=shapes,
                input_output_aliases={known + k: k for k in range(len(filled))},
                compiler_params=pltpu.CompilerParams(vmem_limit_bytes=58 * 1024 * 1024),
                cost_estimate=cost(2 * count * BLOCK * width * (D + 12 * MB), *pieces),
            )(*pieces, *args, *filled, *after)

        half = own_rows // 2
        db_own = d_branch.astype(BF)
        db_a, db_y = swap(db_own, "a"), swap(db_own, "y")
        *filled, gain_part0 = attention_back(6, [db_own, swap(db_own, "c")], (), (down_last,))
        top = swap(ordered(db_y[:half], (gain_part0,)), "a")
        bottom = swap(ordered(db_a[half:], (gain_part0,)), "y")
        far_a, far_y = swap(db_a, "c"), swap(db_y, "c")
        *filled, gain_part1 = attention_back(2, [db_a, far_a, db_y, far_y], filled, ())
        corner = [top, bottom] + [swap(ordered(piece, (gain_part1,)), "c") for piece in (top, bottom)]
        db_all, n_qk, d_value, dots, gain_part2 = attention_back(0, corner, filled, ())
        gu_mine, gu_given = split_rows(grad_gu, y, shard_rows, (gain_part1, top, bottom))
        grad_down_all = lax.all_gather(beside(down_first, down_last, (gu_mine,)), ("a", "c"), axis=0, tiled=True)
        gain_part = jnp.concatenate([gain_part0, gain_part1, gain_part2], axis=0)
        d_gain_query, d_gain_key = jnp.sum(gain_part, axis=0)
        zero = jnp.zeros((D,), F32)
        totals = jnp.concatenate(
            [
                dots.reshape(2, all_rows // D, D).reshape(-1, D),
                lax.dynamic_update_slice(zero, d_gain_query, (pair * width,))[None],
                lax.dynamic_update_slice(zero, d_gain_key, (pair * width,))[None],
                d_gain_attn[None],
                d_gain_mlp[None],
            ]
        )
        for axis, dim in (("a", 1), ("y", 2), ("c", 3)):
            other = swap(totals, axis)
            turned = jnp.flip(other[:-4].reshape(2, 2, 2, 2, own_rows), dim).reshape(-1, D)
            totals = totals + jnp.concatenate([turned, other[-4:]])
            if axis == "a":
                grad_out = weight_grad(attended, db_all, (totals,))[0]
                if planes == 4:
                    out_mine, out_other = exchange_first(grad_out.reshape(planes, -1, D), a)
        dots, gain_terms = totals[:-4].reshape(2, all_rows), totals[-4:]
        d_qkv = call(
            qkv_back_kernel, (blocks,),
            [row_block(2 * width), row_block(2 * width), stat_block(), stat_block(), row_block(width)],
            row_block(3 * width), shaped((all_rows, 3 * width), BF), 0, (n_qk, qkv, squares, dots, d_value),
        )
        gain_rows = jnp.transpose(gain_terms.reshape(4, planes, 2, shard_rows), (1, 2, 0, 3)).reshape(planes, -1)
        more = -(8 * shard_rows) % (3 * width)
        gain_rows = jnp.pad(gain_rows.astype(BF), ((0, 0), (0, more))).reshape(planes, -1, 3 * width)
        gain_rows = jnp.pad(gain_rows, ((0, 0), (0, 16 - gain_rows.shape[1]), (0, 0)))
        grad_qkv_part = weight_grad(x_all, d_qkv, (grad_down_all,), planes, 16)
        grad_qkv = plane_sum(
            lax.dynamic_update_slice(grad_qkv_part, gain_rows, (0, 2 * shard_rows, 0)).reshape(-1, 3 * width)
        )
        own_gains = grad_qkv[2 * shard_rows :].reshape(-1)[: 8 * shard_rows].reshape(2, 4, shard_rows)
        own_gains = lax.dynamic_index_in_dim(own_gains, y, 0, keepdims=False).astype(F32)
        if planes == 4:
            grad_out = exchange_last(out_mine, ordered(out_other, (grad_qkv_part,)), a, c).reshape(width, D)
        gu_near, gu_other = (swap(ordered(piece, (grad_qkv_part,)), axis) for piece, axis in ((gu_mine, "a"), (gu_given, "y")))
        gu_far = swap(gu_other, "a")
        gu_pieces = [gu_mine, gu_other, gu_near, gu_far]
        gu_pieces += [swap(piece, "c") for piece in gu_pieces]
        def column_pair(j, scalars):
            return member_of((j // 2) % 2, j // 4, scalars), scalars[2] ^ (j % 2)

        if quarter % 128 == 0:
            owners = [column_pair(j, scalars) for j in range(8)]
            places = jnp.stack([jnp.stack([(p * 2 + of_y) * 4 + of for p in range(planes)]) for of, of_y in owners])
            grad_gate, grad_up = assemble_hidden(gu_pieces, 8 * ff_here, places.astype(jnp.int32), quarter, planes)
        else:
            filled = jnp.zeros((shard_rows, 2, planes, 2, 4, quarter), F32)
            for j, piece in enumerate(gu_pieces):
                owner, which_y = column_pair(j, scalars)
                piece = piece.astype(F32).reshape(shard_rows, 2, planes, 1, 1, quarter)
                filled = lax.dynamic_update_slice(filled, piece, (0, 0, 0, which_y, owner, 0))
            grad_gate, grad_up = (filled[:, o].reshape(shard_rows, 8 * ff_here) for o in range(2))

        grad_down_full = grad_down_all.astype(F32)
        qkv_mine, qkv_given = split_rows(grad_qkv, y, shard_rows, (grad_gate, grad_down_full))
        qkv_near, qkv_other = swap(qkv_mine, "a"), swap(qkv_given, "y")
        in_parts = []

        def in_part(first, count, after):
            in_parts.append(block_product(d_qkv, qkv_w, first, count, True, after + (grad_qkv_part,)))
            return in_parts[-1]


        d_input, _ = plane_scatter(in_part, lean=True)
        d_input = d_middle + d_input
        if planes == 4:
            grad_out = plane_sum(ordered(grad_out, (grad_qkv, in_parts[2])))

        def qkv_place(o, j, s, scalars):
            owner, which_y = column_pair(j, scalars)
            return 0, owner * 2 + which_y

        qkv_far = swap(qkv_other, "a")
        qkv_pieces = [qkv_mine, qkv_other, qkv_near, qkv_far]
        qkv_pieces += [swap(piece, "c") for piece in qkv_pieces]
        grad_query, grad_key, grad_value = assemble(
            qkv_pieces, [shaped((shard_rows, D), F32)] * 3, shard_rows, width, 1,
            lambda o, s: (0, o), qkv_place, scalars,
        )
        if planes == 4:
            (grad_out,) = assemble(
                spread([grad_out]), [shaped((shard_rows, D), F32)], shard_rows // 4, D, 1,
                lambda o, s: (0, 0), lambda o, j, s, scalars: (member_of(j % 2, j // 2, scalars), 0), scalars,
            )
        else:
            whole = lax.dynamic_update_slice(jnp.zeros((D, D), BF), grad_out, (pair * width, 0))
            whole = lax.psum_scatter(whole, ("z", "y"), scatter_dimension=0, tiled=True)
            grad_out = lax.psum(whole, ("a", "c")).astype(F32)

        return (
            block_output,
            d_input,
            grad_query,
            grad_key,
            grad_value,
            grad_out,
            own_gains[0],
            own_gains[1],
            own_gains[2],
            grad_gate,
            grad_up,
            grad_down_full,
            own_gains[3],
        )

    return body


def solution(mesh):
    replicas, shards = mesh.shape["dp"], mesh.shape["fsdp"]
    planes = shards // 2
    fine = Mesh(mesh.devices.reshape(replicas // 2, 2, planes, 2), ("a", "c", "z", "y"))
    tokens = ("a", "c", "z", "y")
    owner = ("z", "y")
    rows, row, wide, vec = P(tokens, None), P(tokens), P(owner, None), P(owner)
    in_specs = (rows, row, wide, wide, wide, wide, vec, vec, vec, wide, wide, wide, vec, rows)
    out_specs = (rows, rows, wide, wide, wide, wide, vec, vec, vec, wide, wide, wide, vec)
    return jax.shard_map(make_body(planes), mesh=fine, in_specs=in_specs, out_specs=out_specs, check_vma=False)
```

```python
import jax
import jax.numpy as jnp
from jax import lax
from jax.experimental import pallas as pl
from jax.experimental.pallas import tpu as pltpu
from jax.sharding import Mesh, PartitionSpec as P

D = 2048
HEADS = 16
HEAD_DIM = 128
MB = 128
EPS = 1e-06
THETA = 500000.0
NEG = -1e30
BF = jnp.bfloat16
F32 = jnp.float32
SWAP = [(0, 1), (1, 0)]
BLOCK = 256
PARTS = ((0, 2), (2, 4), (6, 2))
VMEM_LIMIT = 40 * 1024 * 1024


def cost(flops, *arrays):
    moved = sum(v.size * v.dtype.itemsize for v in arrays)
    return pl.CostEstimate(flops=flops, bytes_accessed=moved, transcendentals=0)
HALVES = (slice(0, D // 2), slice(D // 2, D))


def product(left_rows, right_rows):
    return jnp.dot(left_rows, right_rows, preferred_element_type=F32)


def product_nt(left_rows, right_rows):
    return lax.dot_general(left_rows, right_rows, (((1,), (1,)), ((), ())), preferred_element_type=F32)


def product_tn(left_rows, right_rows):
    return lax.dot_general(left_rows, right_rows, (((0,), (0,)), ((), ())), preferred_element_type=F32)


def swap(values, axis):
    return lax.ppermute(values, axis, SWAP)


def plane_gather(rows, early=None, hold=()):
    half = rows.shape[0] // 2
    by_a = swap(rows, "a")
    by_y = swap(rows, "y")
    if early is not None:
        early.extend((by_a, by_y))
    top, bottom = by_y[:half], by_a[half:]
    if hold:
        top, bottom = ordered(top, hold), ordered(bottom, hold)
    top = swap(top, "a")
    bottom = swap(bottom, "y")
    far_a, far_y, far_top, far_bottom = (swap(piece, "c") for piece in (by_a, by_y, top, bottom))
    pieces = [top, bottom, far_top, far_bottom, by_a, far_a, by_y, far_y, rows, swap(rows, "c")]
    return jnp.concatenate(pieces, axis=0)


def plane_gather_small(values):
    values = jnp.concatenate([values, swap(values, "c")], axis=0)
    for axis in ("y", "a"):
        values = jnp.concatenate([swap(values, axis), values], axis=0)
    return values


def assemble_hidden(pieces, columns, places, quarter, planes):
    rows, width = pieces[0].shape
    count = len(pieces)
    parts = 2 * planes

    def kernel(places_ref, *refs):
        ins, outs, held, sems = refs[:count], refs[count : count + 2], refs[count + 2], refs[count + 3]

        def copies(k):
            for n in range(parts):
                at = pl.multiple_of(places_ref[k, n % planes] * quarter, quarter)
                yield pltpu.make_async_copy(
                    held.at[k % 2, :, n * quarter : (n + 1) * quarter],
                    outs[n // planes].at[:, pl.ds(at, quarter)],
                    sems.at[k % 2, n],
                )

        for k in range(count):
            if k >= 2:
                for copy in copies(k - 2):
                    copy.wait()
            held[k % 2] = ins[k][...].astype(F32)
            for copy in copies(k):
                copy.start()
        for k in range(count - 2, count):
            for copy in copies(k):
                copy.wait()

    return pl.pallas_call(
        kernel,
        grid_spec=pltpu.PrefetchScalarGridSpec(
            num_scalar_prefetch=1,
            grid=(1,),
            in_specs=[pl.BlockSpec((rows, width), lambda i, s: (0, 0), pipeline_mode=pl.Buffered(1))] * count,
            out_specs=[pl.BlockSpec(memory_space=pl.ANY)] * 2,
            scratch_shapes=[pltpu.VMEM((2, rows, width), F32), pltpu.SemaphoreType.DMA((2, parts))],
        ),
        out_shape=[jax.ShapeDtypeStruct((rows, columns), F32)] * 2,
        compiler_params=pltpu.CompilerParams(vmem_limit_bytes=VMEM_LIMIT),
        cost_estimate=cost(0, *pieces, *pieces, *pieces),
    )(places, *pieces)


def resident(shape):
    return pl.BlockSpec(shape, lambda i: (0,) * len(shape), pipeline_mode=pl.Buffered(1))


def resident_view(view):
    array, rows, columns = view
    return resident((array.shape[0], rows, columns))


def flat(ref):
    value = ref[...]
    return value.reshape(-1, value.shape[-1]) if value.ndim == 3 else value


def row_block(columns, first=0):
    return pl.BlockSpec((BLOCK, columns), lambda i: (first + i, 0))


def stat_block(first=0):
    return pl.BlockSpec((2, BLOCK), lambda i: (0, first + i))


def call(kernel, grid, in_specs, out_specs, out_shape, flops, args, after=(), through=()):
    outs = isinstance(out_shape, (list, tuple))
    out_shape = list(out_shape) if outs else [out_shape]
    out_specs = list(out_specs) if outs else [out_specs]
    extra = len(after) + len(through)
    known = len(args)
    results = len(out_shape)

    def body(*refs):
        kernel(*refs[:known], *refs[known + extra : known + extra + results])

    anywhere = pl.BlockSpec(memory_space=pl.ANY)
    given = pl.pallas_call(
        body,
        grid=grid,
        in_specs=list(in_specs) + [anywhere] * extra,
        out_specs=out_specs + [anywhere] * len(through),
        out_shape=out_shape + [jax.ShapeDtypeStruct(v.shape, v.dtype) for v in through],
        input_output_aliases={known + len(after) + k: results + k for k in range(len(through))},
        compiler_params=pltpu.CompilerParams(vmem_limit_bytes=VMEM_LIMIT),
        cost_estimate=cost(flops, *args, *out_shape),
    )(*args, *after, *through)
    own = given[:results] if outs else given[0]
    return (own, *given[results:]) if through else own


def eye():
    shape = (MB, MB)
    return lax.broadcasted_iota(jnp.int32, shape, 0) == lax.broadcasted_iota(jnp.int32, shape, 1)


def as_column(row):
    return jnp.sum(jnp.where(eye(), row, 0.0), axis=1, keepdims=True)


def as_row(column):
    return jnp.sum(jnp.where(eye(), column, 0.0), axis=0, keepdims=True)


def allowed_pairs(segment_row):
    shape = (MB, MB)
    earlier = lax.broadcasted_iota(jnp.int32, shape, 0) >= lax.broadcasted_iota(jnp.int32, shape, 1)
    return jnp.logical_and(as_column(segment_row) == segment_row, earlier)


def qkv_kernel(x_ref, w_ref, qkv_ref, squares_ref):
    width = w_ref.shape[2] // 3
    qkv = product(x_ref[...], flat(w_ref))
    qkv_ref[...] = qkv
    for kind in range(2):
        part = qkv[:, kind * width : (kind + 1) * width]
        total = jnp.sum(part * part, axis=1, keepdims=True)
        for m in range(BLOCK // MB):
            squares_ref[kind : kind + 1, m * MB : (m + 1) * MB] = as_row(total[m * MB : (m + 1) * MB])


def head_slots(width):
    for m in range(BLOCK // MB):
        for h in range(width // HEAD_DIM):
            starts = [kind * width + h * HEAD_DIM for kind in range(3)]
            yield m, h, slice(m * MB, (m + 1) * MB), [slice(at, at + HEAD_DIM) for at in starts]


def masked_softmax(queries, keys, allowed):
    scores = [product_nt(query, key) * HEAD_DIM**-0.5 for query, key in zip(queries, keys)]
    scores = [jnp.where(mask, score, NEG) for mask, score in zip(allowed, scores)]
    tops = [jnp.max(score, axis=1, keepdims=True) for score in scores]
    powers = [jnp.exp(score - top) for score, top in zip(scores, tops)]
    sums = [jnp.sum(power, axis=1, keepdims=True) for power in powers]
    return [power / total for power, total in zip(powers, sums)]


def attention_kernel(qkv_ref, squares_ref, seg_ref, cos_ref, sin_ref, gain_ref, out_ref, low_ref, att_ref, part_ref):
    width = gain_ref.shape[1]
    scales = lax.rsqrt(squares_ref[...] / D + EPS)
    slots = list(head_slots(width))
    masks, columns = [], []
    for m in range(BLOCK // MB):
        rows = slice(m * MB, (m + 1) * MB)
        masks.append(allowed_pairs(seg_ref[:, rows]))
        columns.append([as_column(scales[kind : kind + 1, rows]) for kind in range(2)])
    lows = [[], [], []]
    for kind in range(2):
        for m, h, rows, ats in slots:
            gain = gain_ref[kind : kind + 1, h * HEAD_DIM : (h + 1) * HEAD_DIM]
            u = qkv_ref[rows, ats[kind]] * columns[m][kind] * gain
            lows[kind].append((u * cos_ref[rows, :] + pltpu.roll(u, HEAD_DIM // 2, 1) * sin_ref[rows, :]).astype(BF))
    lows[2] = [qkv_ref[rows, ats[2]].astype(BF) for m, h, rows, ats in slots]
    probs = masked_softmax(lows[0], lows[1], [masks[m] for m, *_ in slots])
    outs = [product(prob.astype(BF), value).astype(BF) for prob, value in zip(probs, lows[2])]
    for n, (m, h, rows, ats) in enumerate(slots):
        for kind in range(3):
            low_ref[rows, ats[kind]] = lows[kind][n]
        att_ref[rows, h * HEAD_DIM : (h + 1) * HEAD_DIM] = outs[n]
    part_ref[...] = product(att_ref[...], out_ref[...]).astype(BF)


def attention_back_kernel(
    low_ref, qkv_ref, squares_ref, seg_ref, cos_ref, sin_ref, gain_ref, out_ref, db_ref,
    n_ref, dv_ref, dots_ref, gain_part_ref,
):
    width = gain_ref.shape[1]
    scales = lax.rsqrt(squares_ref[...] / D + EPS)
    slots = list(head_slots(width))
    masks, columns = [], []
    for m in range(BLOCK // MB):
        rows = slice(m * MB, (m + 1) * MB)
        masks.append(allowed_pairs(seg_ref[:, rows]))
        columns.append([as_column(scales[kind : kind + 1, rows]) for kind in range(2)])
    queries, keys, values = ([low_ref[rows, ats[kind]] for m, h, rows, ats in slots] for kind in range(3))
    d_att = product_nt(db_ref[...], out_ref[...]).astype(BF)
    d_outs = [d_att[rows, h * HEAD_DIM : (h + 1) * HEAD_DIM] for m, h, rows, ats in slots]
    d_probs = [product_nt(d_out, value) for d_out, value in zip(d_outs, values)]
    probs = masked_softmax(queries, keys, [masks[m] for m, *_ in slots])
    d_values = [product_tn(prob.astype(BF), d_out).astype(BF) for prob, d_out in zip(probs, d_outs)]
    inner = [jnp.sum(prob * d_prob, axis=1, keepdims=True) for prob, d_prob in zip(probs, d_probs)]
    d_scores = [(prob * (d_prob - dot)).astype(BF) for prob, d_prob, dot in zip(probs, d_probs, inner)]
    grads = [
        [product(score, key) for score, key in zip(d_scores, keys)],
        [product_tn(score, query) for score, query in zip(d_scores, queries)],
    ]
    dots = [[jnp.zeros((MB, 1), F32) for _ in range(2)] for _ in range(BLOCK // MB)]
    terms = [[jnp.zeros((1, HEAD_DIM), F32) for _ in range(width // HEAD_DIM)] for _ in range(2)]
    for kind in range(2):
        for n, (m, h, rows, ats) in enumerate(slots):
            u = grads[kind][n] * HEAD_DIM**-0.5
            u = u * cos_ref[rows, :] - pltpu.roll(u, HEAD_DIM // 2, 1) * sin_ref[rows, :]
            raw = qkv_ref[rows, ats[kind]]
            grad = u * gain_ref[kind : kind + 1, h * HEAD_DIM : (h + 1) * HEAD_DIM]
            n_ref[rows, ats[kind]] = grad
            dots[m][kind] += jnp.sum(grad * raw, axis=1, keepdims=True)
            terms[kind][h] += jnp.sum(u * (raw * columns[m][kind]), axis=0, keepdims=True)
    for n, (m, h, rows, ats) in enumerate(slots):
        dv_ref[rows, h * HEAD_DIM : (h + 1) * HEAD_DIM] = d_values[n]
    for kind in range(2):
        for m in range(BLOCK // MB):
            dots_ref[kind : kind + 1, m * MB : (m + 1) * MB] = as_row(dots[m][kind])
        for h in range(width // HEAD_DIM):
            gain_part_ref[0, kind : kind + 1, h * HEAD_DIM : (h + 1) * HEAD_DIM] = terms[kind][h]


def qkv_back_kernel(n_ref, qkv_ref, squares_ref, dots_ref, dv_ref, out_ref):
    width = dv_ref.shape[1]
    scales = lax.rsqrt(squares_ref[...] / D + EPS)
    factors = scales * scales * scales * dots_ref[...] / D
    for m in range(BLOCK // MB):
        rows = slice(m * MB, (m + 1) * MB)
        for kind in range(2):
            at = slice(kind * width, (kind + 1) * width)
            near = as_column(scales[kind : kind + 1, rows])
            far = as_column(factors[kind : kind + 1, rows])
            out_ref[rows, at] = (near * n_ref[rows, at] - far * qkv_ref[rows, at]).astype(BF)
    out_ref[:, 2 * width :] = dv_ref[...]


def gate_up_kernel(mid_ref, w_ref, *refs):
    gate_up_ref, hidden_ref = refs[1:3] if len(refs) > 2 else refs
    if len(refs) > 2:
        refs[3][...] = refs[0][...]
    half = hidden_ref.shape[1]
    both = product(mid_ref[...], flat(w_ref))
    gate, up = both[:, :half], both[:, half:]
    gate_up_ref[...] = both.astype(BF)
    hidden_ref[...] = (gate / (1.0 + jnp.exp(-gate)) * up).astype(BF)


def hidden_back_kernel(dm0_ref, dm1_ref, w0_ref, w1_ref, gate_up_ref, out_ref):
    half = w1_ref.shape[0]
    d_hidden = product_nt(dm0_ref[...], flat(w0_ref)) + product_nt(dm1_ref[...], w1_ref[...])
    gate = gate_up_ref[:, :half].astype(F32)
    up = gate_up_ref[:, half:].astype(F32)
    sig = 1.0 / (1.0 + jnp.exp(-gate))
    out_ref[:, :half] = (d_hidden * up * sig * (1.0 + gate * (1.0 - sig))).astype(BF)
    out_ref[:, half:] = (d_hidden * gate * sig).astype(BF)


def block_product(left, right, first, count, transposed=False, after=()):
    view = isinstance(right, tuple)
    shape = (right[0].shape[0] * right[1], right[2]) if view else right.shape
    columns = shape[0] if transposed else shape[1]

    def kernel(left_ref, right_ref, out_ref):
        out_ref[...] = (product_nt if transposed else product)(left_ref[...], flat(right_ref)).astype(BF)

    return call(
        kernel, (count,),
        [row_block(left.shape[1], first), resident_view(right) if view else resident(right.shape)], row_block(columns),
        jax.ShapeDtypeStruct((count * BLOCK, columns), BF), 2 * count * BLOCK * left.shape[1] * columns,
        (left, right[0] if view else right), after,
    )


def weight_grad(left, right, after=(), parts=1, spare=0):
    rows, columns = left.shape[1] // parts, right.shape[1]
    size = min(BLOCK, rows)
    steps = rows // size

    def kernel(left_ref, right_ref, out_ref):
        out_ref[0] = product_tn(left_ref[...], right_ref[...]).astype(BF)

    return call(
        kernel, (parts * steps,),
        [pl.BlockSpec((left.shape[0], size), lambda i: (0, i)), resident(right.shape)],
        pl.BlockSpec((1, size, columns), lambda i: (i // steps, i % steps, 0)),
        jax.ShapeDtypeStruct((parts, rows + spare, columns), BF), 2 * left.shape[0] * left.shape[1] * columns,
        (left, right), after,
    )


def ordered(values, after):
    def kernel(in_ref, out_ref):
        out_ref[...] = in_ref[...]

    whole = pl.BlockSpec(values.shape, lambda i: (0,) * values.ndim)
    return call(kernel, (1,), [whole], whole, jax.ShapeDtypeStruct(values.shape, values.dtype), 0, (values,), after)


def beside(left, right, after):
    columns = left.shape[1]

    def kernel(left_ref, right_ref, out_ref):
        out_ref[:, :columns] = left_ref[...]
        out_ref[:, columns:] = right_ref[...]

    whole = [pl.BlockSpec(shape, lambda i: (0, 0)) for shape in (left.shape, right.shape)]
    shape = (left.shape[0], columns + right.shape[1])
    return call(
        kernel, (1,), whole, pl.BlockSpec(shape, lambda i: (0, 0)), jax.ShapeDtypeStruct(shape, left.dtype), 0,
        (left, right), after,
    )


def split_rows(values, which, rows, after=()):
    columns = values.shape[1]
    extra = len(after)

    def kernel(which_ref, mine_ref, given_ref, *refs):
        refs[extra][...] = mine_ref[...]
        refs[extra + 1][...] = given_ref[...]

    width = columns // 2
    return pl.pallas_call(
        kernel,
        grid_spec=pltpu.PrefetchScalarGridSpec(
            num_scalar_prefetch=1,
            grid=(2,),
            in_specs=[
                pl.BlockSpec((rows, width), lambda i, w: (w[0], i)),
                pl.BlockSpec((rows, width), lambda i, w: (1 - w[0], i)),
            ]
            + [pl.BlockSpec(memory_space=pl.ANY)] * extra,
            out_specs=[pl.BlockSpec((rows, width), lambda i, w: (0, i))] * 2,
        ),
        out_shape=[jax.ShapeDtypeStruct((rows, columns), values.dtype)] * 2,
        cost_estimate=cost(0, values, values),
    )(jnp.reshape(which, (1,)).astype(jnp.int32), values, values, *after)


def assemble(pieces, out_shape, rows, columns, steps, spots, place, scalars):
    count = len(pieces)
    outs = len(out_shape)

    def in_map(k, o):
        def index(j, s, scalars):
            at = spots(o, jnp.where(j == k, s, jnp.where(j < k, 0, steps - 1)))
            return at

        return index

    def out_map(o):
        return lambda j, s, scalars: place(o, j, s, scalars)

    def kernel(scalar_ref, *refs):
        j = pl.program_id(0)
        for k in range(count):

            @pl.when(j == k)
            def _():
                for o in range(outs):
                    refs[count * outs + o][...] = refs[k * outs + o][...].astype(F32)

    return pl.pallas_call(
        kernel,
        grid_spec=pltpu.PrefetchScalarGridSpec(
            num_scalar_prefetch=1,
            grid=(count, steps),
            in_specs=[pl.BlockSpec((rows, columns), in_map(k, o)) for k in range(count) for o in range(outs)],
            out_specs=[pl.BlockSpec((rows, columns), out_map(o)) for o in range(outs)],
        ),
        out_shape=out_shape,
        compiler_params=pltpu.CompilerParams(vmem_limit_bytes=VMEM_LIMIT),
        cost_estimate=cost(0, *pieces, *out_shape),
    )(scalars, *[p for p in pieces for _ in range(outs)])


def plane_scatter(make, between=None, lean=False):
    corner_part = make(*PARTS[0], ())
    rows = corner_part.shape[0] // 2
    half = rows // 2
    next_part = make(*PARTS[1], (corner_part,))
    corner = (corner_part[:rows].astype(F32) + swap(corner_part[rows:], "c").astype(F32)).astype(BF)
    if between is not None:
        between((corner, next_part))
    if lean:
        from_a, from_y = None, swap(corner, "y").astype(F32)
    else:
        from_a, from_y = swap(corner[:half], "a").astype(F32), swap(corner[half:], "y").astype(F32)
    a_near = next_part[:rows].astype(F32) + swap(next_part[rows : 2 * rows], "c").astype(F32)
    y_near = next_part[2 * rows : 3 * rows].astype(F32) + swap(next_part[3 * rows :], "c").astype(F32)
    if lean:
        to_a, to_y = (a_near + from_y).astype(BF), y_near.astype(BF)
    else:
        to_a = jnp.concatenate([a_near[:half], a_near[half:] + from_y], axis=0).astype(BF)
        to_y = jnp.concatenate([y_near[:half] + from_a, y_near[half:]], axis=0).astype(BF)
    own_part = make(*PARTS[2], (corner, next_part))
    own = own_part[:rows].astype(F32) + swap(own_part[rows:], "c").astype(F32)
    return own + swap(to_a, "a").astype(F32) + swap(to_y, "y").astype(F32), (to_a, to_y)


def plane_sum_tokens(stats):
    kinds, _, count = stats.shape
    values = stats.reshape(kinds, 2, 2, 2, count)
    for axis, dim in (("a", 1), ("y", 2), ("c", 3)):
        values = values + jnp.flip(swap(values, axis), dim)
    return values.reshape(kinds, 8, count)


def exchange_members(blocks, a, c):
    return exchange_last(*exchange_first(blocks, a), a, c)


def exchange_first(blocks, a):
    both = blocks.reshape((2, 2) + blocks.shape[1:])
    mine = lax.dynamic_index_in_dim(both, a, 0, keepdims=False)
    return mine, swap(lax.dynamic_index_in_dim(both, 1 - a, 0, keepdims=False), "a")


def exchange_last(mine, other, a, c):
    blocks = jax.ShapeDtypeStruct((4,) + mine.shape[1:], mine.dtype)
    both = ordered_pair(mine, other, a)
    mine = lax.dynamic_index_in_dim(both, c, 1, keepdims=False)
    other = swap(lax.dynamic_index_in_dim(both, 1 - c, 1, keepdims=False), "c")
    return ordered_pair(mine, other, c, 1).reshape(blocks.shape)


def spread(pieces):
    both = list(pieces) + [swap(piece, "a") for piece in pieces]
    return both + [swap(piece, "c") for piece in both]


def ordered_pair(mine, other, index, axis=0):
    return jnp.where(index == 0, jnp.stack([mine, other], axis=axis), jnp.stack([other, mine], axis=axis))


def rotation_tables(segments):
    row_index = jnp.arange(MB, dtype=jnp.int32)
    same_seg = segments[:, :, None] == segments[:, None, :]
    allowed = jnp.logical_and(same_seg, row_index[:, None] >= row_index[None, :])
    position = jnp.sum(allowed.astype(jnp.int32), axis=2) - 1
    half_dim = HEAD_DIM // 2
    frequency = THETA ** (-2.0 * jnp.arange(half_dim, dtype=F32) / HEAD_DIM)
    angles = position.astype(F32).reshape(-1, 1) * frequency
    cosine, sine = jnp.cos(angles), jnp.sin(angles)
    return jnp.concatenate([cosine, cosine], axis=1), jnp.concatenate([-sine, sine], axis=1)


def make_body(planes):
    def body(
        block_input, segment_ids, w_query, w_key, w_value, w_out, gain_query, gain_key, gain_attn,
        w_gate, w_up, w_down, gain_mlp, out_cotangent,
    ):
        a = lax.axis_index("a")
        c = lax.axis_index("c")
        z = lax.axis_index("z")
        y = lax.axis_index("y")
        member = a * 2 + c
        pair = member * 2 + y
        own_rows = block_input.shape[0]
        all_rows = own_rows * 8
        shard_rows = w_query.shape[0]
        width = D // 8
        ff_shard = w_down.shape[0]
        quarter = ff_shard // 4
        ff_here = planes * quarter
        blocks = all_rows // BLOCK

        segments = plane_gather_small(segment_ids.reshape(own_rows // MB, MB))
        live = (segment_ids >= 0).astype(F32)[:, None]

        def columns_of(which_y):
            at = (member * 2 + which_y) * width
            return jnp.concatenate(
                [lax.dynamic_slice(w, (0, at), (shard_rows, width)) for w in (w_query, w_key, w_value)], axis=1
            )

        def hidden_columns_of(which_y):
            starts = [((plane * 2 + which_y) * 4 + member) * quarter for plane in range(planes)]
            return jnp.concatenate(
                [lax.dynamic_slice(w, (0, at), (shard_rows, quarter)) for w in (w_gate, w_up) for at in starts], axis=1
            )

        def column_weights(mine, given, more, next_to=()):
            both = ordered_pair(mine, swap(given, "y"), y).reshape(2 * shard_rows, -1)
            return jnp.concatenate([jnp.concatenate([both] + list(next_to), axis=1), more], axis=0)

        def gather_planes(piece):
            return lax.all_gather(piece, "z", axis=0, tiled=False)

        own_gains = jnp.stack([gain_query, gain_key, gain_attn, gain_mlp]).reshape(2, 2 * shard_rows)
        more, next_to = own_gains, []
        if planes == 4:
            out_piece = lax.dynamic_slice(w_out, (member * (shard_rows // 4), 0), (shard_rows // 4, D))
            next_to = [out_piece.reshape(2 * shard_rows, -1)]
        more = jnp.pad(own_gains, ((0, 14), (0, (3 + len(next_to)) * width - 2 * shard_rows)))
        qkv_array = gather_planes(column_weights(columns_of(y), columns_of(1 - y), more, next_to))
        x_near = []
        x_all = plane_gather(block_input, x_near)
        down_pieces = [lax.dynamic_slice(w_down, (member * quarter, n * D // 2), (quarter, D // 2)) for n in range(2)]
        gu_given = ordered(hidden_columns_of(1 - y), x_near)
        gu_array = gather_planes(
            column_weights(
                hidden_columns_of(y), gu_given,
                jnp.concatenate([down_pieces[0][: quarter // 2], down_pieces[0][quarter // 2 :]], axis=1),
            )
        )
        last_down = gather_planes(down_pieces[1]).reshape(ff_here, D // 2)
        qkv_w = (qkv_array, 2 * shard_rows, 3 * width)
        gains = qkv_array[:, 2 * shard_rows : 2 * shard_rows + 2, : 2 * shard_rows].reshape(planes, 4, shard_rows)
        gains = ordered_pair(gains, swap(gains, "y"), y, 1)
        gains = jnp.transpose(gains, (2, 0, 1, 3)).reshape(4, D).astype(F32)
        gain_q = lax.dynamic_slice(gains[0], (pair * width,), (width,))
        gain_k = lax.dynamic_slice(gains[1], (pair * width,), (width,))
        gain_a, gain_m = gains[2], gains[3]
        if planes == 4:
            out_pieces = qkv_array[:, : 2 * shard_rows, 3 * width :].reshape(planes, shard_rows // 4, D)
            out_rows = exchange_members(out_pieces, a, c).reshape(width, D)
        else:
            out_rows = lax.dynamic_slice(
                lax.all_gather(w_out, ("z", "y"), axis=0, tiled=True), (pair * width, 0), (width, D)
            )
        gu_w = (gu_array, 2 * shard_rows, 2 * ff_here)

        shaped = jax.ShapeDtypeStruct
        cosine, sine = rotation_tables(segments)
        qkv, squares = call(
            qkv_kernel, (blocks,), [row_block(D), resident_view(qkv_w)], [row_block(3 * width), stat_block()],
            [shaped((all_rows, 3 * width), F32), shaped((2, all_rows), F32)], 2 * all_rows * D * 3 * width,
            (x_all, qkv_array), (cosine, sine),
        )
        squares = plane_sum_tokens(squares.reshape(2, 8, own_rows)).reshape(2, all_rows)
        seg_row = segments.astype(F32).reshape(1, all_rows)
        gain_qk = jnp.stack([gain_q, gain_k])

        def attention(first, count, after):
            return call(
                attention_kernel, (count,),
                [
                    row_block(3 * width, first), stat_block(first), pl.BlockSpec((1, BLOCK), lambda i: (0, first + i)),
                    row_block(HEAD_DIM, first), row_block(HEAD_DIM, first), resident((2, width)), resident((width, D)),
                ],
                [row_block(3 * width), row_block(width), row_block(D)],
                [shaped((count * BLOCK, cols), BF) for cols in (3 * width, width, D)],
                2 * count * BLOCK * width * (D + 2 * MB),
                (qkv, squares, seg_row, cosine, sine, gain_qk, out_rows), after,
            )

        lows, atts = [], []

        def branch_part(first, count, after):
            low_part, att_part, part = attention(first, count, after)
            lows.append(low_part)
            atts.append(att_part)
            return part

        branch, _ = plane_scatter(branch_part)
        attended = jnp.concatenate(atts, axis=0)
        low = jnp.concatenate(lows, axis=0)

        def row_scale(values):
            return lax.rsqrt(jnp.mean(values * values, axis=-1, keepdims=True) + EPS)

        def norm_back(values, scale_here, gain, upstream):
            n = upstream * gain
            grad = scale_here * n - scale_here**3 * values * jnp.mean(n * values, axis=-1, keepdims=True)
            return grad, jnp.sum(upstream * values * scale_here, axis=0)

        branch_scale = row_scale(branch)
        middle = block_input.astype(F32) + branch * branch_scale * gain_a
        mid_all = plane_gather(middle.astype(BF))

        size, first = quarter // 2, 2 * shard_rows // (quarter // 2)
        half_in = pl.BlockSpec((1, size, D // 2), lambda i: (i // 2, first, i % 2))
        half_out = pl.BlockSpec((1, size, D // 2), lambda i: (i // 2, i % 2, 0))
        half_shape = shaped((planes, quarter, D // 2), BF)
        together = blocks == 2 * planes
        gate_up, hidden, *first_down = call(
            gate_up_kernel, (blocks,), [row_block(D), resident_view(gu_w)] + [half_in] * together,
            [row_block(2 * ff_here), row_block(ff_here)] + [half_out] * together,
            [shaped((all_rows, 2 * ff_here), BF), shaped((all_rows, ff_here), BF)] + [half_shape] * together,
            4 * all_rows * D * ff_here, (mid_all, gu_array) + (gu_array,) * together,
        )
        if not together:

            def take_kernel(in_ref, out_ref):
                out_ref[...] = in_ref[...]

            first_down = call(take_kernel, (2 * planes,), [half_in], [half_out], [half_shape], 0, (gu_array,), (hidden,))
        down_w = [first_down[0].reshape(ff_here, D // 2), last_down]
        mixed0, marks = plane_scatter(lambda first, count, after: block_product(hidden, down_w[0], first, count, False, after))
        mixed1, _ = plane_scatter(
            lambda first, count, after: block_product(hidden, down_w[1], first, count, False, after + marks)
        )
        mixed = jnp.concatenate([mixed0, mixed1], axis=1)
        mixed_scale = row_scale(mixed)
        block_output = ((middle + mixed * mixed_scale * gain_m) * live).astype(BF)

        grad_rows = out_cotangent.astype(F32) * live
        d_mixed, d_gain_mlp = norm_back(mixed, mixed_scale, gain_m, grad_rows)
        early = []
        dm_halves = [d_mixed[:, cut].astype(BF) for cut in HALVES]
        dm_all = [plane_gather(dm_halves[0], early)]
        grad_down_parts = [product_tn(hidden, dm_all[0]).astype(BF)]
        dm_all.append(plane_gather(ordered(dm_halves[1], early)))
        grad_down_parts = grad_down_parts + [product_tn(hidden, dm_all[1]).astype(BF)]

        def plane_sum(values):
            return lax.psum_scatter(values.astype(BF), "z", scatter_dimension=0, tiled=True)

        grad_down = [plane_sum(part) for part in grad_down_parts]
        d_gu = call(
            hidden_back_kernel, (blocks,),
            [row_block(D // 2), row_block(D // 2), resident((ff_here, D // 2)), resident((ff_here, D // 2)),
             row_block(2 * ff_here)],
            row_block(2 * ff_here), shaped((all_rows, 2 * ff_here), BF), 2 * all_rows * D * ff_here,
            (*dm_all, *down_w, gate_up), grad_down_parts[:1],
        )
        down_first = ordered(grad_down[0], (d_gu,))
        grad_gu_part = weight_grad(mid_all, d_gu, (down_first,))[0]
        grad_gu = plane_sum(grad_gu_part)
        d_middle, _ = plane_scatter(
            lambda first, count, after: block_product(d_gu, gu_w, first, count, True, after + (grad_gu_part,))
        )
        scalars = jnp.stack([a, c, y]).astype(jnp.int32)

        def member_of(j_a, j_c, scalars):
            return (scalars[0] ^ j_a) * 2 + (scalars[1] ^ j_c)

        d_middle = grad_rows + d_middle
        down_last = ordered(grad_down[1], (d_middle,))

        d_branch, d_gain_attn = norm_back(branch, branch_scale, gain_a, d_middle)
        def attention_back(first, pieces, filled, after):
            places = []
            for piece in pieces:
                places.append((sum(p.shape[0] for p in pieces[: len(places)]), piece.shape[0]))
            count = sum(rows for _, rows in places) // BLOCK

            def kernel(*refs):
                ins, rest = refs[: len(pieces)], refs[len(pieces) :]
                db_ref = rest[8 + len(filled)]
                for (start, rows), ref in zip(places, ins):

                    @pl.when(pl.program_id(0) == start // BLOCK)
                    def _():
                        db_ref[start % BLOCK : start % BLOCK + rows, :] = ref[...]

                attention_back_kernel(*rest[:8], *rest[8 + len(filled) :])

            return call_back(kernel, first, count, pieces, filled, after)

        def call_back(kernel, first, count, pieces, filled, after):
            known = len(pieces) + 8
            shapes = [
                shaped((all_rows, D), BF), shaped((all_rows, 2 * width), F32), shaped((all_rows, width), BF),
                shaped((2, all_rows), F32), shaped((count, 2, width), F32),
            ]
            anywhere = pl.BlockSpec(memory_space=pl.ANY)
            args = (low, qkv, squares, seg_row, cosine, sine, gain_qk, out_rows)
            extra = len(after)

            def body(*refs):
                kernel(*refs[: known + len(filled)], *refs[known + len(filled) + extra :])

            return pl.pallas_call(
                body,
                grid=(count,),
                in_specs=[resident(piece.shape) for piece in pieces]
                + [
                    row_block(3 * width, first), row_block(2 * width, first), stat_block(first),
                    pl.BlockSpec((1, BLOCK), lambda i: (0, first + i)), row_block(HEAD_DIM, first),
                    row_block(HEAD_DIM, first), resident((2, width)), resident((width, D)),
                ]
                + [anywhere] * (len(filled) + extra),
                out_specs=[
                    row_block(D, first), row_block(2 * width, first), row_block(width, first), stat_block(first),
                    pl.BlockSpec((1, 2, width), lambda i: (i, 0, 0)),
                ],
                out_shape=shapes,
                input_output_aliases={known + k: k for k in range(len(filled))},
                compiler_params=pltpu.CompilerParams(vmem_limit_bytes=58 * 1024 * 1024),
                cost_estimate=cost(2 * count * BLOCK * width * (D + 12 * MB), *pieces),
            )(*pieces, *args, *filled, *after)

        half = own_rows // 2
        db_own = d_branch.astype(BF)
        db_a, db_y = swap(db_own, "a"), swap(db_own, "y")
        *filled, gain_part0 = attention_back(6, [db_own, swap(db_own, "c")], (), (down_last,))
        top = swap(ordered(db_y[:half], (gain_part0,)), "a")
        bottom = swap(ordered(db_a[half:], (gain_part0,)), "y")
        far_a, far_y = swap(db_a, "c"), swap(db_y, "c")
        *filled, gain_part1 = attention_back(2, [db_a, far_a, db_y, far_y], filled, ())
        corner = [top, bottom] + [swap(ordered(piece, (gain_part1,)), "c") for piece in (top, bottom)]
        db_all, n_qk, d_value, dots, gain_part2 = attention_back(0, corner, filled, ())
        gu_mine, gu_given = split_rows(grad_gu, y, shard_rows, (gain_part1, top, bottom))
        grad_down_all = lax.all_gather(beside(down_first, down_last, (gu_mine,)), ("a", "c"), axis=0, tiled=True)
        gain_part = jnp.concatenate([gain_part0, gain_part1, gain_part2], axis=0)
        d_gain_query, d_gain_key = jnp.sum(gain_part, axis=0)
        zero = jnp.zeros((D,), F32)
        totals = jnp.concatenate(
            [
                dots.reshape(2, all_rows // D, D).reshape(-1, D),
                lax.dynamic_update_slice(zero, d_gain_query, (pair * width,))[None],
                lax.dynamic_update_slice(zero, d_gain_key, (pair * width,))[None],
                d_gain_attn[None],
                d_gain_mlp[None],
            ]
        )
        for axis, dim in (("a", 1), ("y", 2), ("c", 3)):
            other = swap(totals, axis)
            turned = jnp.flip(other[:-4].reshape(2, 2, 2, 2, own_rows), dim).reshape(-1, D)
            totals = totals + jnp.concatenate([turned, other[-4:]])
            if axis == "a":
                grad_out = weight_grad(attended, db_all, (totals,))[0]
                if planes == 4:
                    out_mine, out_other = exchange_first(grad_out.reshape(planes, -1, D), a)
        dots, gain_terms = totals[:-4].reshape(2, all_rows), totals[-4:]
        d_qkv = call(
            qkv_back_kernel, (blocks,),
            [row_block(2 * width), row_block(2 * width), stat_block(), stat_block(), row_block(width)],
            row_block(3 * width), shaped((all_rows, 3 * width), BF), 0, (n_qk, qkv, squares, dots, d_value),
        )
        gain_rows = jnp.transpose(gain_terms.reshape(4, planes, 2, shard_rows), (1, 2, 0, 3)).reshape(planes, -1)
        more = -(8 * shard_rows) % (3 * width)
        gain_rows = jnp.pad(gain_rows.astype(BF), ((0, 0), (0, more))).reshape(planes, -1, 3 * width)
        gain_rows = jnp.pad(gain_rows, ((0, 0), (0, 16 - gain_rows.shape[1]), (0, 0)))
        grad_qkv_part = weight_grad(x_all, d_qkv, (grad_down_all,), planes, 16)
        grad_qkv = plane_sum(
            lax.dynamic_update_slice(grad_qkv_part, gain_rows, (0, 2 * shard_rows, 0)).reshape(-1, 3 * width)
        )
        own_gains = grad_qkv[2 * shard_rows :].reshape(-1)[: 8 * shard_rows].reshape(2, 4, shard_rows)
        own_gains = lax.dynamic_index_in_dim(own_gains, y, 0, keepdims=False).astype(F32)
        if planes == 4:
            grad_out = exchange_last(out_mine, ordered(out_other, (grad_qkv_part,)), a, c).reshape(width, D)
        gu_near, gu_other = (swap(ordered(piece, (grad_qkv_part,)), axis) for piece, axis in ((gu_mine, "a"), (gu_given, "y")))
        gu_far = swap(gu_other, "a")
        gu_pieces = [gu_mine, gu_other, gu_near, gu_far]
        gu_pieces += [swap(piece, "c") for piece in gu_pieces]
        def column_pair(j, scalars):
            return member_of((j // 2) % 2, j // 4, scalars), scalars[2] ^ (j % 2)

        if quarter % 128 == 0:
            owners = [column_pair(j, scalars) for j in range(8)]
            places = jnp.stack([jnp.stack([(p * 2 + of_y) * 4 + of for p in range(planes)]) for of, of_y in owners])
            grad_gate, grad_up = assemble_hidden(gu_pieces, 8 * ff_here, places.astype(jnp.int32), quarter, planes)
        else:
            filled = jnp.zeros((shard_rows, 2, planes, 2, 4, quarter), F32)
            for j, piece in enumerate(gu_pieces):
                owner, which_y = column_pair(j, scalars)
                piece = piece.astype(F32).reshape(shard_rows, 2, planes, 1, 1, quarter)
                filled = lax.dynamic_update_slice(filled, piece, (0, 0, 0, which_y, owner, 0))
            grad_gate, grad_up = (filled[:, o].reshape(shard_rows, 8 * ff_here) for o in range(2))

        grad_down_full = grad_down_all.astype(F32)
        qkv_mine, qkv_given = split_rows(grad_qkv, y, shard_rows, (grad_gate, grad_down_full))
        qkv_near, qkv_other = swap(qkv_mine, "a"), swap(qkv_given, "y")
        in_parts = []

        def in_part(first, count, after):
            in_parts.append(block_product(d_qkv, qkv_w, first, count, True, after + (grad_qkv_part,)))
            return in_parts[-1]


        d_input, _ = plane_scatter(in_part, lean=True)
        d_input = d_middle + d_input
        if planes == 4:
            grad_out = plane_sum(ordered(grad_out, (grad_qkv, in_parts[2])))

        def qkv_place(o, j, s, scalars):
            owner, which_y = column_pair(j, scalars)
            return 0, owner * 2 + which_y

        qkv_far = swap(qkv_other, "a")
        qkv_pieces = [qkv_mine, qkv_other, qkv_near, qkv_far]
        qkv_pieces += [swap(piece, "c") for piece in qkv_pieces]
        grad_query, grad_key, grad_value = assemble(
            qkv_pieces, [shaped((shard_rows, D), F32)] * 3, shard_rows, width, 1,
            lambda o, s: (0, o), qkv_place, scalars,
        )
        if planes == 4:
            (grad_out,) = assemble(
                spread([grad_out]), [shaped((shard_rows, D), F32)], shard_rows // 4, D, 1,
                lambda o, s: (0, 0), lambda o, j, s, scalars: (member_of(j % 2, j // 2, scalars), 0), scalars,
            )
        else:
            whole = lax.dynamic_update_slice(jnp.zeros((D, D), BF), grad_out, (pair * width, 0))
            whole = lax.psum_scatter(whole, ("z", "y"), scatter_dimension=0, tiled=True)
            grad_out = lax.psum(whole, ("a", "c")).astype(F32)

        return (
            block_output,
            d_input,
            grad_query,
            grad_key,
            grad_value,
            grad_out,
            own_gains[0],
            own_gains[1],
            own_gains[2],
            grad_gate,
            grad_up,
            grad_down_full,
            own_gains[3],
        )

    return body


def solution(mesh):
    replicas, shards = mesh.shape["dp"], mesh.shape["fsdp"]
    planes = shards // 2
    fine = Mesh(mesh.devices.reshape(replicas // 2, 2, planes, 2), ("a", "c", "z", "y"))
    tokens = ("a", "c", "z", "y")
    owner = ("z", "y")
    rows, row, wide, vec = P(tokens, None), P(tokens), P(owner, None), P(owner)
    in_specs = (rows, row, wide, wide, wide, wide, vec, vec, vec, wide, wide, wide, vec, rows)
    out_specs = (rows, rows, wide, wide, wide, wide, vec, vec, vec, wide, wide, wide, vec)
    return jax.shard_map(make_body(planes), mesh=fine, in_specs=in_specs, out_specs=out_specs, check_vma=False)
```
